512 devices in a mesh: ta: 16 (over y, core), gz: 8 (over z), gy: 4 (over x).
Axes of the slice: x: 4, y: 8, z: 8, core: 2. Of those that a mesh axis runs over, the one named last changes fastest.
Arguments:
- residual: bfloat16 [2, 4, 3, 16, 16, 8, 4, 512], P(None, None, None, None, 'ta', 'gz', 'gy'), may hold values from -40 to 40
- null_vectors: bfloat16 [2, 24, 4, 3, 16, 8, 4, 512], P(None, None, None, None, 'ta', 'gz', 'gy'), may hold values from -0.078125 to 0.078125
- coarse_op: bfloat16 [16, 8, 4, 9, 2, 48, 48], P(None, 'gz', 'gy'), may hold values from -1 to 1
Outputs:
- correction: bfloat16 [2, 4, 3, 16, 16, 8, 4, 512], P(None, None, None, None, 'ta', 'gz', 'gy')
- coarse_residual: float32 [2, 48, 16, 8, 4, 16], P(None, None, 'ta', 'gz', 'gy')
The draws below stay inside these ranges and needn't reach their ends.
All inputs are finite; a program needn't handle non-finite values.
Results may differ from the reference program's by a relative error of at most 0.009.
Values may be sent and summed in bfloat16 or wider, within the bound.
A program may use at most 64 MiB of HBM per device.

```python
import math
import jax
import jax.numpy as jnp
from jax import lax

NVEC = 24
CDOF = 48
SITES = 512
NRHS = 16
ITERS = 4
TSLABS = 16
ZSLABS = 8
YSLABS = 4


def draw_residual(key, part):
    key = jax.random.fold_in(key, 11)
    shape = (2, 4, 3, NRHS, TSLABS, ZSLABS, YSLABS, SITES)
    first, second = jax.random.split(key)
    values = jax.random.truncated_normal(first, -6.0, 6.0, shape, jnp.float32)
    ramp_rate = 0.55
    zpos = lax.broadcasted_iota(jnp.float32, shape, 5)
    ypos = lax.broadcasted_iota(jnp.float32, shape, 6)
    ramp = (zpos * YSLABS + ypos) / max(ZSLABS * YSLABS - 1, 1)
    column_scale = jnp.exp(jax.random.uniform(second, (NRHS,), jnp.float32, -1.15, 1.15))
    return (values * jnp.exp(ramp_rate * ramp) * column_scale.reshape(1, 1, 1, NRHS, 1, 1, 1, 1)).astype(jnp.bfloat16)


def draw_coarse_op(key, part):
    key = jax.random.fold_in(key, 23)
    shape = (TSLABS, ZSLABS, YSLABS, 9, 2, CDOF, CDOF)
    first, second = jax.random.split(key)
    sigma = 0.012 / math.sqrt(CDOF)
    noise = jax.random.truncated_normal(first, -6.0, 6.0, shape, jnp.float32) * sigma
    diagonal = 0.1 * jnp.exp(jax.random.uniform(second, (TSLABS, ZSLABS, YSLABS, CDOF), jnp.float32, -0.7, 0.7))
    link = lax.broadcasted_iota(jnp.int32, shape, 3)
    parity = lax.broadcasted_iota(jnp.int32, shape, 4)
    row_index = lax.broadcasted_iota(jnp.int32, shape, 5)
    col_index = lax.broadcasted_iota(jnp.int32, shape, 6)
    on_diagonal = ((link == 0) & (parity == 0) & (row_index == col_index)).astype(jnp.float32)
    return (noise + on_diagonal * diagonal[:, :, :, None, None, :, None]).astype(jnp.bfloat16)


def levels(own_key, extent, pieces, smallest, largest):
    def one(axis_at, parts):
        heights = jax.random.uniform(jax.random.fold_in(jax.random.fold_in(own_key, 6), axis_at), (parts,), jnp.float32, smallest / len(pieces), largest / len(pieces))
        return jnp.repeat(jnp.exp(heights), extent[axis_at] // parts).reshape((-1,) + (1,) * (len(extent) - axis_at - 1))

    level = one(*pieces[0])
    for cut in pieces[1:]:
        level = level * one(*cut)
    return level


def normal_values(stream_key, shape, scale, most, cuts=(), kind=jnp.bfloat16):
    factor_of = levels(stream_key, shape, cuts, -0.22, 0.18) if cuts else 1.0
    array = jax.random.normal(stream_key, shape, jnp.float32) * scale * factor_of
    return jnp.minimum(jnp.maximum(array, -most), most).astype(kind)


def setup_inputs(seed: int = 0) -> dict:
    arg_keys = jax.random.split(jax.random.key(seed), 4)
    return {
        "residual": draw_residual(jax.random.fold_in(arg_keys[3], 71), 0),
        "null_vectors": normal_values(arg_keys[1], (2, NVEC, 4, 3, TSLABS, ZSLABS, YSLABS, SITES), (12 * SITES) ** -0.5, 0.078125, ((4, 16), (5, 8), (6, 4))),
        "coarse_op": draw_coarse_op(jax.random.fold_in(arg_keys[3], 71), 0),
    }


HIGH = lax.Precision.HIGHEST


def restrict_slab(basis, source):
    nvec = basis.shape[1]
    zcount, ycount, sites = basis.shape[4], basis.shape[5], basis.shape[6]
    rhs = source.shape[3]
    basis = basis.astype(jnp.float32).reshape(2, nvec, 2, 2, 3, zcount, ycount, sites)
    source = source.astype(jnp.float32).reshape(2, 2, 2, 3, rhs, zcount, ycount, sites)
    prod = jnp.einsum("pkcabzys,qcabrzys->pqckzyr", basis, source, precision=HIGH)
    real = (prod[0, 0] + prod[1, 1]).reshape(2 * nvec, zcount, ycount, rhs)
    imag = (prod[0, 1] - prod[1, 0]).reshape(2 * nvec, zcount, ycount, rhs)
    return jnp.stack([real, imag])


def prolong_slab(basis, coarse):
    nvec = basis.shape[1]
    zcount, ycount, sites = basis.shape[4], basis.shape[5], basis.shape[6]
    rhs = coarse.shape[-1]
    basis = basis.astype(jnp.float32).reshape(2, nvec, 2, 2, 3, zcount, ycount, sites)
    coarse = coarse.astype(jnp.float32).reshape(2, 2, nvec, zcount, ycount, rhs)
    prod = jnp.einsum("pkcabzys,qckzyr->pqcabrzys", basis, coarse, precision=HIGH)
    real = (prod[0, 0] - prod[1, 1]).reshape(4, 3, rhs, zcount, ycount, sites)
    imag = (prod[0, 1] + prod[1, 0]).reshape(4, 3, rhs, zcount, ycount, sites)
    return jnp.stack([real, imag]).astype(jnp.bfloat16)


def contract(left, right):
    return jnp.einsum("tzymij,mjtzyr->itzyr", left, right, precision=HIGH)


def apply_links(links, stacked):
    lreal = links[:, :, :, :, 0]
    limag = links[:, :, :, :, 1]
    real = contract(lreal, stacked[:, 0]) - contract(limag, stacked[:, 1])
    imag = contract(lreal, stacked[:, 1]) + contract(limag, stacked[:, 0])
    return jnp.stack([real, imag])


def operate(links, field):
    stacked = jnp.stack([field,
                         jnp.roll(field, -1, 2), jnp.roll(field, 1, 2),
                         jnp.roll(field, -1, 3), jnp.roll(field, 1, 3),
                         jnp.roll(field, -1, 4), jnp.roll(field, 1, 4),
                         field, field])
    return apply_links(links, stacked)


def inner(left, right):
    real = jnp.sum(left[0] * right[0] + left[1] * right[1], axis=(0, 1, 2, 3))
    imag = jnp.sum(left[0] * right[1] - left[1] * right[0], axis=(0, 1, 2, 3))
    return real, imag


def cscale(sreal, simag, field):
    return jnp.stack([sreal * field[0] - simag * field[1], sreal * field[1] + simag * field[0]])


def reference(residual, null_vectors, coarse_op):
    slab_ids = jnp.arange(TSLABS, dtype=jnp.int32)

    def restrict_one(index):
        basis = lax.dynamic_index_in_dim(null_vectors, index, 4, keepdims=False)
        source = lax.dynamic_index_in_dim(residual, index, 4, keepdims=False)
        return restrict_slab(basis, source)

    restricted = jnp.moveaxis(lax.map(restrict_one, slab_ids), 0, 2)
    links = coarse_op.astype(jnp.float32)
    solution = jnp.zeros_like(restricted)
    remain = restricted
    kept_q = []
    kept_p = []
    kept_n = []
    for step in range(ITERS):
        search = remain
        image = operate(links, search)
        products = [inner(prior, image) for prior in kept_q]
        for j in range(len(kept_q)):
            breal = products[j][0] / kept_n[j]
            bimag = products[j][1] / kept_n[j]
            image = image - cscale(breal, bimag, kept_q[j])
            search = search - cscale(breal, bimag, kept_p[j])
        square = inner(image, image)[0]
        creal, cimag = inner(image, remain)
        areal = creal / square
        aimag = cimag / square
        solution = solution + cscale(areal, aimag, search)
        remain = remain - cscale(areal, aimag, image)
        kept_q.append(image)
        kept_p.append(search)
        kept_n.append(square)
    rounded = solution.astype(jnp.bfloat16)

    def prolong_one(index):
        basis = lax.dynamic_index_in_dim(null_vectors, index, 4, keepdims=False)
        coarse = lax.dynamic_index_in_dim(rounded, index, 2, keepdims=False)
        return prolong_slab(basis, coarse)

    correction = jnp.moveaxis(lax.map(prolong_one, slab_ids), 0, 4)
    return correction, remain
```

```python
import functools

import jax
import jax.numpy as jnp
from jax import lax
from jax.experimental import pallas as pl
from jax.experimental.pallas import tpu as pltpu
from jax.sharding import PartitionSpec as P

MESH = pl.DeviceIdType.MESH
F32 = jnp.float32
BF16 = jnp.bfloat16
CDOF = 48
NVEC = 24
NRHS = 16
LINKS = 9
LANES = 128


def lane_iota(shape):
    return lax.broadcasted_iota(jnp.int32, shape, len(shape) - 1)


def group_of(shape):
    return lax.rem(lax.div(lane_iota(shape), NRHS), 4)


def sign_of(shape):
    return jnp.where(lane_iota(shape) < 64, -1.0, 1.0).astype(F32)


def times_i(field):
    return sign_of(field.shape) * pltpu.roll(field, 64, 1)


def restrict(nv_ref, res_ref, rows_ref):
    total = None
    for colour in range(3):
        basis = nv_ref[:, :, colour].reshape(2 * NVEC * 4, 512)
        source = res_ref[:, :, colour].reshape(2 * 4 * NRHS, 512)
        part = lax.dot_general(basis, source, (((1,), (1,)), ((), ())), preferred_element_type=F32)
        total = part if total is None else total + part
    rows_ref[...] = total
    by_spin = [rows_ref[pl.ds(s, 2 * NVEC, stride=4), :] for s in range(4)]
    group = group_of((2 * NVEC, LANES))
    halves = []
    for chirality in range(2):
        a, b = 2 * chirality, 2 * chirality + 1
        picked = jnp.where(group == a, by_spin[a], jnp.where(group == b, by_spin[b], 0.0))
        picked = picked + pltpu.roll(picked, LANES - NRHS, 1)
        if chirality == 1:
            picked = pltpu.roll(picked, LANES - 2 * NRHS, 1)
        halves.append(picked[:NVEC] - times_i(picked[NVEC:]))
    field = jnp.concatenate(halves, axis=0)
    return jnp.where(group == 0, field, 0.0)


def packed(field):
    high = field.astype(BF16).astype(F32)
    return (high + pltpu.roll(field - high, 2 * NRHS, 1)).astype(BF16)


def apply_links(links, cells):
    product = jnp.dot(links, cells, preferred_element_type=F32)
    value = product[:CDOF] + times_i(product[CDOF:])
    value = value + pltpu.roll(value, LANES - 2 * NRHS, 1)
    return jnp.where(group_of(value.shape) == 0, value, 0.0)


def row_sum(product):
    return jnp.sum(product, axis=0, keepdims=True)


def cmul(a, b):
    return a[0] * b[0] - a[1] * b[1], a[0] * b[1] + a[1] * b[0]


def cmul_conj(a, b):
    return a[0] * b[0] + a[1] * b[1], a[0] * b[1] - a[1] * b[0]


def csub(a, b):
    return a[0] - b[0], a[1] - b[1]


def solve(diag, upper, right):
    n = len(diag)
    d, inv, low = [], [], {}
    for j in range(n):
        value = diag[j]
        for k in range(j):
            value = value - d[k] * (low[j, k][0] ** 2 + low[j, k][1] ** 2)
        d.append(value)
        inv.append(1.0 / value)
        for i in range(j + 1, n):
            entry = (upper[j, i][0], -upper[j, i][1])
            for k in range(j):
                term = cmul_conj(low[j, k], low[i, k])
                entry = csub(entry, (d[k] * term[0], d[k] * term[1]))
            low[i, j] = (entry[0] * inv[j], entry[1] * inv[j])
    y = []
    for i in range(n):
        value = right[i]
        for k in range(i):
            value = csub(value, cmul(low[i, k], y[k]))
        y.append(value)
    c = [None] * n
    for i in reversed(range(n)):
        value = (y[i][0] * inv[i], y[i][1] * inv[i])
        for k in range(i + 1, n):
            value = csub(value, cmul_conj(low[k, i], c[k]))
        c[i] = value
    return c


def both_halves(row):
    row = jnp.where(lane_iota(row.shape) < NRHS, row, 0.0)
    return row + pltpu.roll(row, 64, 1)


def all_to_all(shape, me, peers, value, buf, send_sem, recv_sem):
    buf[me] = value
    for peer in peers:
        pltpu.make_async_remote_copy(
            src_ref=buf.at[me],
            dst_ref=buf.at[me],
            send_sem=send_sem,
            recv_sem=recv_sem,
            device_id=peer,
            device_id_type=MESH,
        ).start()


def all_wait(count, peer, buf, send_sem, recv_sem):
    block = buf.at[pl.ds(0, count)]
    arrived = pltpu.make_async_remote_copy(
        src_ref=block, dst_ref=block, send_sem=send_sem, recv_sem=recv_sem, device_id=peer, device_id_type=MESH
    )
    arrived.wait_recv()
    arrived.wait_send()


def coarse_kernel(
    sizes,
    res_hbm,
    nv_hbm,
    op_hbm,
    x_ref,
    r_ref,
    res_v,
    nv_v,
    op_v,
    col_v,
    rows_v,
    cells,
    theta_buf,
    t_buf,
    zx_buf,
    local_sem,
    halo_send,
    halo_recv,
    sum_send,
    sum_recv,
):
    nt, nz, nx = sizes
    t, z, x = lax.axis_index("ta"), lax.axis_index("gz"), lax.axis_index("gy")
    loads = [
        pltpu.make_async_copy(op_hbm.at[t, 0, 0], op_v, local_sem.at[0]),
        pltpu.make_async_copy(op_hbm.at[:, 0, 0, 0], col_v, local_sem.at[1]),
        pltpu.make_async_copy(res_hbm, res_v, local_sem.at[2]),
        pltpu.make_async_copy(nv_hbm, nv_v, local_sem.at[3]),
    ]
    for load in loads:
        load.start()
    t_peers = [(lax.rem(t + d, nt), z, x) for d in range(1, nt)]
    zx_peers = [
        (t, lax.rem(z + a, nz), lax.rem(x + b, nx)) for a in range(nz) for b in range(nx) if (a, b) != (0, 0)
    ]
    barrier = pltpu.get_barrier_semaphore()
    for peer in t_peers + zx_peers:
        pl.semaphore_signal(barrier, inc=1, device_id=peer, device_id_type=MESH)

    loads[1].wait()
    eye = lax.broadcasted_iota(jnp.int32, (CDOF, CDOF), 0) == lax.broadcasted_iota(jnp.int32, (CDOF, CDOF), 1)
    trace = [jnp.zeros((CDOF, CDOF), F32), jnp.zeros((CDOF, CDOF), F32)]
    square = jnp.zeros((CDOF, CDOF), F32)
    for slab in range(nt):
        for part in range(2):
            block = col_v[slab, part].astype(F32)
            trace[part] = trace[part] + block
            square = square + block * block
    scale = 1.0 / (nt * nz * nx * CDOF)
    stats = [jnp.where(eye, trace[0], 0.0), jnp.where(eye, trace[1], 0.0), square]
    stats = [jnp.sum(row_sum(value), axis=1, keepdims=True) * scale for value in stats]
    stats = jnp.concatenate([jnp.broadcast_to(value, (1, LANES)) for value in stats], axis=0)

    loads[0].wait()
    links = jnp.concatenate(
        [
            jnp.concatenate([op_v[m, part].astype(F32) for m in range(LINKS)], axis=1)
            for part in range(2)
        ],
        axis=0,
    ).astype(BF16)

    loads[2].wait()
    loads[3].wait()
    start = restrict(nv_v, res_v, rows_v)
    pl.semaphore_wait(barrier, len(t_peers) + len(zx_peers))

    slots = [
        (1, (lax.rem(t + nt - 1, nt), z, x)),
        (2, (lax.rem(t + 1, nt), z, x)),
        (3, (t, lax.rem(z + nz - 1, nz), x)),
        (4, (t, lax.rem(z + 1, nz), x)),
        (5, (t, z, lax.rem(x + nx - 1, nx))),
        (6, (t, z, lax.rem(x + 1, nx))),
    ]
    me_zx = z * nx + x
    powers = [start]
    for k in range(4):
        own = packed(powers[k])
        cells[k, 0] = own
        for m, peer in slots:
            pltpu.make_async_remote_copy(
                src_ref=cells.at[k, 0],
                dst_ref=cells.at[k, m],
                send_sem=halo_send.at[k],
                recv_sem=halo_recv.at[k],
                device_id=peer,
                device_id_type=MESH,
            ).start()
        cells[k, 7] = own
        cells[k, 8] = own
        if k == 0:
            all_to_all(None, me_zx, zx_peers, stats, theta_buf, sum_send.at[0], sum_recv.at[0])
        six = cells.at[k, pl.ds(1, 6)]
        arrived = pltpu.make_async_remote_copy(
            src_ref=six,
            dst_ref=six,
            send_sem=halo_send.at[k],
            recv_sem=halo_recv.at[k],
            device_id=slots[0][1],
            device_id_type=MESH,
        )
        arrived.wait_recv()
        arrived.wait_send()
        powers.append(apply_links(links, cells[k].reshape(LINKS * CDOF, LANES)))

    all_wait(nz * nx - 1, zx_peers[0], theta_buf, sum_send.at[0], sum_recv.at[0])
    stats = jnp.sum(theta_buf[...], axis=0)
    square = stats[2:3]
    inverse = jnp.where(square > 0.0, lax.rsqrt(jnp.where(square > 0.0, square, 1.0)), 1.0)
    theta = (stats[0:1] * inverse, stats[1:2] * inverse)

    level = []
    weight = None
    for k in range(5):
        level.append(powers[k] if k == 0 else powers[k] * weight)
        weight = inverse if weight is None else weight * inverse
    basis = [level[0]]
    for _ in range(4):
        level = [
            level[i + 1] - theta[0] * level[i] - theta[1] * times_i(level[i]) for i in range(len(level) - 1)
        ]
        basis.append(level[0])
    images = [
        basis[k + 1] + theta[0] * basis[k] + theta[1] * times_i(basis[k]) for k in range(4)
    ]
    turned = [times_i(image) for image in images]
    start_turned = times_i(start)

    pairs = [(i, j) for i in range(4) for j in range(i + 1, 4)]
    rows = [row_sum(images[k] * images[k]) for k in range(4)]
    rows += [row_sum(images[k] * start) for k in range(4)]
    rows += [row_sum(turned[k] * start) for k in range(4)]
    rows += [row_sum(images[i] * images[j]) for i, j in pairs]
    rows += [row_sum(turned[i] * images[j]) for i, j in pairs]
    table = jnp.concatenate(rows, axis=0)
    table = table + pltpu.roll(table, 64, 1)
    table = jnp.where(lane_iota(table.shape) < NRHS, table, 0.0)
    dense = jnp.concatenate(
        [
            row_sum(pltpu.roll(table[8 * g : 8 * g + 8], 0, 1, stride=NRHS, stride_axis=0))
            for g in range(3)
        ],
        axis=0,
    )

    all_to_all(None, t, t_peers, dense, t_buf, sum_send.at[1], sum_recv.at[1])
    all_wait(nt - 1, t_peers[0], t_buf, sum_send.at[1], sum_recv.at[1])
    dense = jnp.sum(t_buf[...], axis=0)
    all_to_all(None, me_zx, zx_peers, dense, zx_buf, sum_send.at[2], sum_recv.at[2])
    all_wait(nz * nx - 1, zx_peers[0], zx_buf, sum_send.at[2], sum_recv.at[2])
    dense = jnp.sum(zx_buf[...], axis=0)

    sums = []
    for g in range(3):
        spread = pltpu.roll(
            jnp.broadcast_to(dense[g : g + 1], (8, LANES)), 0, 1, stride=NRHS, stride_axis=0
        )
        sums += [spread[(8 - i) % 8 : (8 - i) % 8 + 1] for i in range(8)]
    diag = sums[0:4]
    right = [(sums[4 + k], sums[8 + k]) for k in range(4)]
    upper = {pair: (sums[12 + n], sums[18 + n]) for n, pair in enumerate(pairs)}
    coef = [(both_halves(c[0]), both_halves(c[1])) for c in solve(diag, upper, right)]

    field = None
    remain = start
    for k in range(4):
        cr, ci = coef[k]
        term = (cr * basis[k] + ci * times_i(basis[k])) * inverse
        field = term if field is None else field + term
        remain = remain - cr * images[k] - ci * turned[k]
    x_ref[...] = field
    r_ref[...] = remain


def prolong_kernel(x_ref, r_ref, nv_ref, out_ref, remain_ref, rows_v):
    x = x_ref[...].astype(BF16).astype(F32)
    upper, lower = x[:NVEC], x[NVEC:]
    every = upper + pltpu.roll(upper, NRHS, 1) + pltpu.roll(lower, 2 * NRHS, 1) + pltpu.roll(lower, 3 * NRHS, 1)
    every = jnp.concatenate([every, times_i(every)], axis=0)
    group = group_of(every.shape)
    for s in range(4):
        rows_v[pl.ds(s, 2 * NVEC, stride=4), :] = jnp.where(group == s, every, 0.0)
    weights = rows_v[...].T.astype(BF16)
    for colour in range(3):
        basis = nv_ref[:, :, colour].reshape(2 * NVEC * 4, 512)
        value = jnp.dot(weights, basis, preferred_element_type=F32)
        out_ref[:, :, colour] = value.astype(BF16).reshape(2, 4, NRHS, 512)
    turned = r_ref[...].T
    remain_ref[0] = turned[0:NRHS]
    remain_ref[1] = turned[64 : 64 + NRHS]


def body(sizes, residual, null_vectors, coarse_op):
    sites = residual.shape[-1]
    res = residual.reshape(2, 4, 3, NRHS, sites)
    nv = null_vectors.transpose(0, 1, 3, 4, 5, 6, 2, 7).reshape(2, NVEC, 3, 4, sites)
    nt, nz, nx = sizes
    any_spec = pl.BlockSpec(memory_space=pltpu.HBM)
    vmem_spec = pl.BlockSpec(memory_space=pltpu.VMEM)
    field = jax.ShapeDtypeStruct((CDOF, LANES), F32)
    x, r = pl.pallas_call(
        functools.partial(coarse_kernel, sizes),
        out_shape=(field, field),
        in_specs=[any_spec] * 3,
        out_specs=(vmem_spec, vmem_spec),
        scratch_shapes=[
            pltpu.VMEM(res.shape, BF16),
            pltpu.VMEM(nv.shape, BF16),
            pltpu.VMEM((LINKS, 2, CDOF, CDOF), BF16),
            pltpu.VMEM((nt, 2, CDOF, CDOF), BF16),
            pltpu.VMEM((2 * NVEC * 4, LANES), F32),
            pltpu.VMEM((4, LINKS, CDOF, LANES), BF16),
            pltpu.VMEM((nz * nx, 3, LANES), F32),
            pltpu.VMEM((nt, 3, LANES), F32),
            pltpu.VMEM((nz * nx, 3, LANES), F32),
            pltpu.SemaphoreType.DMA((4,)),
            pltpu.SemaphoreType.DMA((4,)),
            pltpu.SemaphoreType.DMA((4,)),
            pltpu.SemaphoreType.DMA((3,)),
            pltpu.SemaphoreType.DMA((3,)),
        ],
        compiler_params=pltpu.CompilerParams(
            collective_id=0, has_side_effects=True, vmem_limit_bytes=16 * 1024 * 1024
        ),
    )(res, nv, coarse_op)
    correction, remain = pl.pallas_call(
        prolong_kernel,
        out_shape=(
            jax.ShapeDtypeStruct((2, 4, 3, NRHS, sites), BF16),
            jax.ShapeDtypeStruct((2, NRHS, CDOF), F32),
        ),
        in_specs=[vmem_spec] * 3,
        out_specs=(vmem_spec, vmem_spec),
        scratch_shapes=[pltpu.VMEM((2 * NVEC * 4, LANES), F32)],
        compiler_params=pltpu.CompilerParams(vmem_limit_bytes=16 * 1024 * 1024),
    )(x, r, nv)
    correction = correction.reshape(2, 4, 3, NRHS, 1, 1, 1, sites)
    remain = remain.transpose(0, 2, 1).reshape(2, CDOF, 1, 1, 1, NRHS)
    return correction, remain


def solution(mesh):
    sizes = (mesh.shape["ta"], mesh.shape["gz"], mesh.shape["gy"])
    return jax.shard_map(
        functools.partial(body, sizes),
        mesh=mesh,
        in_specs=(
            P(None, None, None, None, "ta", "gz", "gy", None),
            P(None, None, None, None, "ta", "gz", "gy", None),
            P(None, "gz", "gy", None, None, None, None),
        ),
        out_specs=(
            P(None, None, None, None, "ta", "gz", "gy", None),
            P(None, None, "ta", "gz", "gy", None),
        ),
        check_vma=False,
    )
```

```python
import functools

import jax
import jax.numpy as jnp
from jax import lax
from jax.experimental import pallas as pl
from jax.experimental.pallas import tpu as pltpu
from jax.sharding import PartitionSpec as P

MESH = pl.DeviceIdType.MESH
F32 = jnp.float32
BF16 = jnp.bfloat16
CDOF = 48
NVEC = 24
NRHS = 16
LINKS = 9
LANES = 128


def lane_iota(shape):
    return lax.broadcasted_iota(jnp.int32, shape, len(shape) - 1)


def group_of(shape):
    return lax.rem(lax.div(lane_iota(shape), NRHS), 4)


def sign_of(shape):
    return jnp.where(lane_iota(shape) < 64, -1.0, 1.0).astype(F32)


def times_i(field):
    return sign_of(field.shape) * pltpu.roll(field, 64, 1)


def restrict(nv_ref, res_ref, rows_ref):
    total = None
    for colour in range(3):
        basis = nv_ref[:, :, colour].reshape(2 * NVEC * 4, 512)
        source = res_ref[:, :, colour].reshape(2 * 4 * NRHS, 512)
        part = lax.dot_general(basis, source, (((1,), (1,)), ((), ())), preferred_element_type=F32)
        total = part if total is None else total + part
    rows_ref[...] = total
    by_spin = [rows_ref[pl.ds(s, 2 * NVEC, stride=4), :] for s in range(4)]
    group = group_of((2 * NVEC, LANES))
    halves = []
    for chirality in range(2):
        a, b = 2 * chirality, 2 * chirality + 1
        picked = jnp.where(group == a, by_spin[a], jnp.where(group == b, by_spin[b], 0.0))
        picked = picked + pltpu.roll(picked, LANES - NRHS, 1)
        if chirality == 1:
            picked = pltpu.roll(picked, LANES - 2 * NRHS, 1)
        halves.append(picked[:NVEC] - times_i(picked[NVEC:]))
    field = jnp.concatenate(halves, axis=0)
    return jnp.where(group == 0, field, 0.0)


def packed(field):
    high = field.astype(BF16).astype(F32)
    return (high + pltpu.roll(field - high, 2 * NRHS, 1)).astype(BF16)


def apply_links(links, cells):
    product = jnp.dot(links, cells, preferred_element_type=F32)
    value = product[:CDOF] + times_i(product[CDOF:])
    value = value + pltpu.roll(value, LANES - 2 * NRHS, 1)
    return jnp.where(group_of(value.shape) == 0, value, 0.0)


def row_sum(product):
    return jnp.sum(product, axis=0, keepdims=True)


def cmul(a, b):
    return a[0] * b[0] - a[1] * b[1], a[0] * b[1] + a[1] * b[0]


def cmul_conj(a, b):
    return a[0] * b[0] + a[1] * b[1], a[0] * b[1] - a[1] * b[0]


def csub(a, b):
    return a[0] - b[0], a[1] - b[1]


def solve(diag, upper, right):
    n = len(diag)
    d, inv, low = [], [], {}
    for j in range(n):
        value = diag[j]
        for k in range(j):
            value = value - d[k] * (low[j, k][0] ** 2 + low[j, k][1] ** 2)
        d.append(value)
        inv.append(1.0 / value)
        for i in range(j + 1, n):
            entry = (upper[j, i][0], -upper[j, i][1])
            for k in range(j):
                term = cmul_conj(low[j, k], low[i, k])
                entry = csub(entry, (d[k] * term[0], d[k] * term[1]))
            low[i, j] = (entry[0] * inv[j], entry[1] * inv[j])
    y = []
    for i in range(n):
        value = right[i]
        for k in range(i):
            value = csub(value, cmul(low[i, k], y[k]))
        y.append(value)
    c = [None] * n
    for i in reversed(range(n)):
        value = (y[i][0] * inv[i], y[i][1] * inv[i])
        for k in range(i + 1, n):
            value = csub(value, cmul_conj(low[k, i], c[k]))
        c[i] = value
    return c


def both_halves(row):
    row = jnp.where(lane_iota(row.shape) < NRHS, row, 0.0)
    return row + pltpu.roll(row, 64, 1)


def others(count, me):
    return [k + jnp.where(k >= me, 1, 0) for k in range(count - 1)]


def send_to_all(me, peers, value, buf, send_sem, recv_sem):
    buf[me] = value
    for peer in peers:
        pltpu.make_async_remote_copy(
            src_ref=buf.at[me],
            dst_ref=buf.at[me],
            send_sem=send_sem,
            recv_sem=recv_sem,
            device_id=peer,
            device_id_type=MESH,
        ).start()


def transfers(block, peer, send_sem, recv_sem):
    return pltpu.make_async_remote_copy(
        src_ref=block, dst_ref=block, send_sem=send_sem, recv_sem=recv_sem, device_id=peer, device_id_type=MESH
    )


def coarse_kernel(
    sizes,
    res_hbm,
    nv_hbm,
    op_hbm,
    x_ref,
    r_ref,
    res_v,
    nv_v,
    op_v,
    col_v,
    rows_v,
    cells,
    theta_buf,
    t_buf,
    zx_buf,
    local_sem,
    halo_send,
    halo_recv,
    sum_send,
    sum_recv,
):
    nt, nz, nx = sizes
    t, z, x = lax.axis_index("ta"), lax.axis_index("gz"), lax.axis_index("gy")
    me_zx = z * nx + x
    loads = [
        pltpu.make_async_copy(nv_hbm, nv_v, local_sem.at[0]),
        pltpu.make_async_copy(res_hbm, res_v, local_sem.at[1]),
        pltpu.make_async_copy(op_hbm.at[t, 0, 0], op_v, local_sem.at[2]),
        pltpu.make_async_copy(op_hbm.at[:, 0, 0, 0], col_v, local_sem.at[3]),
    ]
    slots = [
        (3, (t, lax.rem(z + nz - 1, nz), x)),
        (4, (t, lax.rem(z + 1, nz), x)),
        (5, (t, z, lax.rem(x + nx - 1, nx))),
        (6, (t, z, lax.rem(x + 1, nx))),
        (1, (lax.rem(t + nt - 1, nt), z, x)),
        (2, (lax.rem(t + 1, nt), z, x)),
    ]
    far = [(lax.rem(t + d, nt), z, x) for d in range(2, nt - 1)]
    far += [
        (t, lax.rem(z + a, nz), lax.rem(x + b, nx))
        for a in range(nz)
        for b in range(nx)
        if (a, b) not in ((0, 0), (1, 0), (nz - 1, 0), (0, 1), (0, nx - 1))
    ]
    barrier = pltpu.get_barrier_semaphore()
    for load in loads[:2]:
        load.start()
    for _, peer in slots:
        pl.semaphore_signal(barrier, inc=1, device_id=peer, device_id_type=MESH)
    for load in loads[2:]:
        load.start()
    for peer in far:
        pl.semaphore_signal(barrier, inc=1, device_id=peer, device_id_type=MESH)
    t_peers = [(k, z, x) for k in others(nt, t)]
    zx_peers = [(t, lax.div(k, nx), lax.rem(k, nx)) for k in others(nz * nx, me_zx)]

    loads[0].wait()
    loads[1].wait()
    start = restrict(nv_v, res_v, rows_v)
    pl.semaphore_wait(barrier, len(slots) + len(far))

    def send_halo(k, field):
        own = packed(field)
        cells[k, 0] = own
        for m, peer in slots:
            pltpu.make_async_remote_copy(
                src_ref=cells.at[k, 0],
                dst_ref=cells.at[k, m],
                send_sem=halo_send.at[k],
                recv_sem=halo_recv.at[k],
                device_id=peer,
                device_id_type=MESH,
            ).start()
        cells[k, 7] = own
        cells[k, 8] = own

    def halo(k):
        return transfers(cells.at[k, pl.ds(1, 6)], slots[0][1], halo_send.at[k], halo_recv.at[k])

    def sums_of(k, buf, count, peer):
        return transfers(buf.at[pl.ds(0, count - 1)], peer, sum_send.at[k], sum_recv.at[k])

    send_halo(0, start)

    loads[3].wait()
    eye = lax.broadcasted_iota(jnp.int32, (CDOF, CDOF), 0) == lax.broadcasted_iota(jnp.int32, (CDOF, CDOF), 1)
    trace = [jnp.zeros((CDOF, CDOF), F32), jnp.zeros((CDOF, CDOF), F32)]
    square = jnp.zeros((CDOF, CDOF), F32)
    for slab in range(nt):
        for part in range(2):
            block = col_v[slab, part].astype(F32)
            trace[part] = trace[part] + block
            square = square + block * block
    scale = 1.0 / (nt * nz * nx * CDOF)
    stats = [jnp.where(eye, trace[0], 0.0), jnp.where(eye, trace[1], 0.0), square]
    stats = [jnp.sum(row_sum(value), axis=1, keepdims=True) * scale for value in stats]
    stats = jnp.concatenate([jnp.broadcast_to(value, (1, LANES)) for value in stats], axis=0)
    send_to_all(me_zx, zx_peers, stats, theta_buf, sum_send.at[0], sum_recv.at[0])

    loads[2].wait()
    links = jnp.concatenate(
        [
            jnp.concatenate([op_v[m, part].astype(F32) for m in range(LINKS)], axis=1)
            for part in range(2)
        ],
        axis=0,
    ).astype(BF16)

    powers = [start]
    for k in range(3):
        halo(k).wait_recv()
        powers.append(apply_links(links, cells[k].reshape(LINKS * CDOF, LANES)))
        send_halo(k + 1, powers[k + 1])

    sums_of(0, theta_buf, nz * nx, zx_peers[0]).wait_recv()
    stats = jnp.sum(theta_buf[...], axis=0)
    square = stats[2:3]
    inverse = jnp.where(square > 0.0, lax.rsqrt(jnp.where(square > 0.0, square, 1.0)), 1.0)
    theta = (stats[0:1] * inverse, stats[1:2] * inverse)
    weights = [inverse]
    for _ in range(3):
        weights.append(weights[-1] * inverse)

    def times_theta(field):
        return theta[0] * field + theta[1] * times_i(field)

    level = [start] + [powers[k] * weights[k - 1] for k in range(1, 4)]
    basis, last = [start], [times_theta(level[3])]
    for _ in range(3):
        level = [level[i + 1] - times_theta(level[i]) for i in range(len(level) - 1)]
        basis.append(level[0])
        last.append(times_theta(level[-1]))
    images = [basis[k + 1] + times_theta(basis[k]) for k in range(3)]
    turned = [times_i(image) for image in images]
    start_turned = times_i(start)

    pairs = [(i, j) for j in range(4) for i in range(j)]
    norms = [row_sum(images[k] * images[k]) for k in range(3)]
    right = [row_sum(images[k] * start) for k in range(3)]
    right_i = [row_sum(turned[k] * start) for k in range(3)]
    cross = [row_sum(images[i] * images[j]) for i, j in pairs[:3]]
    cross_i = [row_sum(turned[i] * images[j]) for i, j in pairs[:3]]

    halo(3).wait_recv()
    newest = apply_links(links, cells[3].reshape(LINKS * CDOF, LANES)) * weights[3]
    for part in last:
        newest = newest - part
    images.append(newest + last[3])
    norms.append(row_sum(images[3] * images[3]))
    right.append(row_sum(images[3] * start))
    right_i.append(-row_sum(images[3] * start_turned))
    cross += [row_sum(images[i] * images[3]) for i in range(3)]
    cross_i += [row_sum(turned[i] * images[3]) for i in range(3)]
    table = jnp.concatenate(norms + right + right_i + cross + cross_i, axis=0)
    table = table + pltpu.roll(table, 64, 1)
    table = jnp.where(lane_iota(table.shape) < NRHS, table, 0.0)
    dense = jnp.concatenate(
        [
            row_sum(pltpu.roll(table[8 * g : 8 * g + 8], 0, 1, stride=NRHS, stride_axis=0))
            for g in range(3)
        ],
        axis=0,
    )

    send_to_all(t, t_peers, dense, t_buf, sum_send.at[1], sum_recv.at[1])
    turned.append(times_i(images[3]))
    basis_turned = [times_i(field) for field in basis]
    sums_of(1, t_buf, nt, t_peers[0]).wait_recv()
    dense = jnp.sum(t_buf[...], axis=0)
    send_to_all(me_zx, zx_peers, dense, zx_buf, sum_send.at[2], sum_recv.at[2])
    sums_of(2, zx_buf, nz * nx, zx_peers[0]).wait_recv()
    dense = jnp.sum(zx_buf[...], axis=0)

    sums = []
    for g in range(3):
        spread = pltpu.roll(jnp.broadcast_to(dense[g : g + 1], (8, LANES)), 0, 1, stride=NRHS, stride_axis=0)
        sums += [spread[(8 - i) % 8 : (8 - i) % 8 + 1] for i in range(8)]
    diag = sums[0:4]
    right = [(sums[4 + k], sums[8 + k]) for k in range(4)]
    upper = {pair: (sums[12 + n], sums[18 + n]) for n, pair in enumerate(pairs)}
    coef = [(both_halves(c[0]), both_halves(c[1])) for c in solve(diag, upper, right)]

    field = None
    remain = start
    for k in range(4):
        cr, ci = coef[k]
        term = (cr * basis[k] + ci * basis_turned[k]) * inverse
        field = term if field is None else field + term
        remain = remain - cr * images[k] - ci * turned[k]
    x_ref[...] = field
    r_ref[...] = remain

    for k in range(4):
        halo(k).wait_send()
    sums_of(0, theta_buf, nz * nx, zx_peers[0]).wait_send()
    sums_of(1, t_buf, nt, t_peers[0]).wait_send()
    sums_of(2, zx_buf, nz * nx, zx_peers[0]).wait_send()


def prolong_kernel(x_ref, r_ref, nv_ref, out_ref, remain_ref, rows_v):
    x = x_ref[...].astype(BF16).astype(F32)
    upper, lower = x[:NVEC], x[NVEC:]
    every = upper + pltpu.roll(upper, NRHS, 1) + pltpu.roll(lower, 2 * NRHS, 1) + pltpu.roll(lower, 3 * NRHS, 1)
    every = jnp.concatenate([every, times_i(every)], axis=0)
    group = group_of(every.shape)
    for s in range(4):
        rows_v[pl.ds(s, 2 * NVEC, stride=4), :] = jnp.where(group == s, every, 0.0)
    weights = rows_v[...].T.astype(BF16)
    for colour in range(3):
        basis = nv_ref[:, :, colour].reshape(2 * NVEC * 4, 512)
        value = jnp.dot(weights, basis, preferred_element_type=F32)
        out_ref[:, :, colour] = value.astype(BF16).reshape(2, 4, NRHS, 512)
    turned = r_ref[...].T
    remain_ref[0] = turned[0:NRHS]
    remain_ref[1] = turned[64 : 64 + NRHS]


def body(sizes, residual, null_vectors, coarse_op):
    sites = residual.shape[-1]
    res = residual.reshape(2, 4, 3, NRHS, sites)
    nv = null_vectors.transpose(0, 1, 3, 4, 5, 6, 2, 7).reshape(2, NVEC, 3, 4, sites)
    nt, nz, nx = sizes
    any_spec = pl.BlockSpec(memory_space=pltpu.HBM)
    vmem_spec = pl.BlockSpec(memory_space=pltpu.VMEM)
    field = jax.ShapeDtypeStruct((CDOF, LANES), F32)
    far = [pltpu.with_memory_space_constraint(a, pltpu.HBM) for a in (res, nv, coarse_op)]
    x, r = pl.pallas_call(
        functools.partial(coarse_kernel, sizes),
        out_shape=(field, field),
        in_specs=[any_spec] * 3,
        out_specs=(vmem_spec, vmem_spec),
        scratch_shapes=[
            pltpu.VMEM(res.shape, BF16),
            pltpu.VMEM(nv.shape, BF16),
            pltpu.VMEM((LINKS, 2, CDOF, CDOF), BF16),
            pltpu.VMEM((nt, 2, CDOF, CDOF), BF16),
            pltpu.VMEM((2 * NVEC * 4, LANES), F32),
            pltpu.VMEM((4, LINKS, CDOF, LANES), BF16),
            pltpu.VMEM((nz * nx, 3, LANES), F32),
            pltpu.VMEM((nt, 3, LANES), F32),
            pltpu.VMEM((nz * nx, 3, LANES), F32),
            pltpu.SemaphoreType.DMA((4,)),
            pltpu.SemaphoreType.DMA((4,)),
            pltpu.SemaphoreType.DMA((4,)),
            pltpu.SemaphoreType.DMA((3,)),
            pltpu.SemaphoreType.DMA((3,)),
        ],
        compiler_params=pltpu.CompilerParams(
            collective_id=0, has_side_effects=True, vmem_limit_bytes=16 * 1024 * 1024
        ),
    )(*far)
    correction, remain = pl.pallas_call(
        prolong_kernel,
        out_shape=(
            jax.ShapeDtypeStruct((2, 4, 3, NRHS, sites), BF16),
            jax.ShapeDtypeStruct((2, NRHS, CDOF), F32),
        ),
        in_specs=[vmem_spec] * 3,
        out_specs=(vmem_spec, vmem_spec),
        scratch_shapes=[pltpu.VMEM((2 * NVEC * 4, LANES), F32)],
        compiler_params=pltpu.CompilerParams(vmem_limit_bytes=16 * 1024 * 1024),
    )(x, r, nv)
    correction = correction.reshape(2, 4, 3, NRHS, 1, 1, 1, sites)
    remain = remain.transpose(0, 2, 1).reshape(2, CDOF, 1, 1, 1, NRHS)
    return correction, remain


def solution(mesh):
    sizes = (mesh.shape["ta"], mesh.shape["gz"], mesh.shape["gy"])
    return jax.shard_map(
        functools.partial(body, sizes),
        mesh=mesh,
        in_specs=(
            P(None, None, None, None, "ta", "gz", "gy", None),
            P(None, None, None, None, "ta", "gz", "gy", None),
            P(None, "gz", "gy", None, None, None, None),
        ),
        out_specs=(
            P(None, None, None, None, "ta", "gz", "gy", None),
            P(None, None, "ta", "gz", "gy", None),
        ),
        check_vma=False,
    )
```

```python
import functools

import jax
import jax.numpy as jnp
from jax import lax
from jax.experimental import pallas as pl
from jax.experimental.pallas import tpu as pltpu
from jax.sharding import PartitionSpec as P

MESH = pl.DeviceIdType.MESH
F32 = jnp.float32
BF16 = jnp.bfloat16
CDOF = 48
NVEC = 24
NRHS = 16
LINKS = 9
LANES = 128


def lane_iota(shape):
    return lax.broadcasted_iota(jnp.int32, shape, len(shape) - 1)


def group_of(shape):
    return lax.rem(lax.div(lane_iota(shape), NRHS), 4)


def sign_of(shape):
    return jnp.where(lane_iota(shape) < 64, -1.0, 1.0).astype(F32)


def times_i(field):
    return sign_of(field.shape) * pltpu.roll(field, 64, 1)


def restrict(nv_ref, res_ref, rows_ref):
    total = None
    for colour in range(3):
        basis = nv_ref[:, :, colour].reshape(2 * NVEC * 4, 512)
        source = res_ref[:, :, colour].reshape(2 * 4 * NRHS, 512)
        part = lax.dot_general(basis, source, (((1,), (1,)), ((), ())), preferred_element_type=F32)
        total = part if total is None else total + part
    rows_ref[...] = total
    by_spin = [rows_ref[pl.ds(s, 2 * NVEC, stride=4), :] for s in range(4)]
    group = group_of((2 * NVEC, LANES))
    halves = []
    for chirality in range(2):
        a, b = 2 * chirality, 2 * chirality + 1
        picked = jnp.where(group == a, by_spin[a], jnp.where(group == b, by_spin[b], 0.0))
        picked = picked + pltpu.roll(picked, LANES - NRHS, 1)
        if chirality == 1:
            picked = pltpu.roll(picked, LANES - 2 * NRHS, 1)
        halves.append(picked[:NVEC] - times_i(picked[NVEC:]))
    field = jnp.concatenate(halves, axis=0)
    return jnp.where(group == 0, field, 0.0)


def packed(field):
    high = field.astype(BF16).astype(F32)
    return (high + pltpu.roll(field - high, 2 * NRHS, 1)).astype(BF16)


def apply_links(links, cells):
    product = jnp.dot(links, cells, preferred_element_type=F32)
    value = product[:CDOF] + times_i(product[CDOF:])
    value = value + pltpu.roll(value, LANES - 2 * NRHS, 1)
    return jnp.where(group_of(value.shape) == 0, value, 0.0)


def row_sum(product):
    return jnp.sum(product, axis=0, keepdims=True)


def cmul(a, b):
    return a[0] * b[0] - a[1] * b[1], a[0] * b[1] + a[1] * b[0]


def cmul_conj(a, b):
    return a[0] * b[0] + a[1] * b[1], a[0] * b[1] - a[1] * b[0]


def csub(a, b):
    return a[0] - b[0], a[1] - b[1]


def solve(diag, upper, right):
    n = len(diag)
    d, inv, low = [], [], {}
    for j in range(n):
        value = diag[j]
        for k in range(j):
            value = value - d[k] * (low[j, k][0] ** 2 + low[j, k][1] ** 2)
        d.append(value)
        inv.append(1.0 / value)
        for i in range(j + 1, n):
            entry = (upper[j, i][0], -upper[j, i][1])
            for k in range(j):
                term = cmul_conj(low[j, k], low[i, k])
                entry = csub(entry, (d[k] * term[0], d[k] * term[1]))
            low[i, j] = (entry[0] * inv[j], entry[1] * inv[j])
    y = []
    for i in range(n):
        value = right[i]
        for k in range(i):
            value = csub(value, cmul(low[i, k], y[k]))
        y.append(value)
    c = [None] * n
    for i in reversed(range(n)):
        value = (y[i][0] * inv[i], y[i][1] * inv[i])
        for k in range(i + 1, n):
            value = csub(value, cmul_conj(low[k, i], c[k]))
        c[i] = value
    return c


def both_halves(row):
    row = jnp.where(lane_iota(row.shape) < NRHS, row, 0.0)
    return row + pltpu.roll(row, 64, 1)


def others(count, me):
    return [k + jnp.where(k >= me, 1, 0) for k in range(count - 1)]


def rank_of(t, nt):
    half = nt // 2
    y = lax.div(t, 2)
    r = jnp.where(y == 0, 0, jnp.where(y <= half // 2, 2 * y - 1, 2 * (half - y)))
    return 2 * r + lax.rem(t, 2)


def slab_of(rank, nt):
    half = nt // 2
    r = lax.div(rank, 2)
    y = jnp.where(lax.rem(r, 2) == 1, lax.div(r + 1, 2), lax.rem(half - lax.div(r, 2), half))
    return 2 * y + lax.rem(rank, 2)


def send_to_all(me, peers, value, buf, send_sem, recv_sem):
    buf[me] = value
    for peer in peers:
        pltpu.make_async_remote_copy(
            src_ref=buf.at[me],
            dst_ref=buf.at[me],
            send_sem=send_sem,
            recv_sem=recv_sem,
            device_id=peer,
            device_id_type=MESH,
        ).start()


def transfers(block, peer, send_sem, recv_sem):
    return pltpu.make_async_remote_copy(
        src_ref=block, dst_ref=block, send_sem=send_sem, recv_sem=recv_sem, device_id=peer, device_id_type=MESH
    )


def coarse_kernel(
    sizes,
    res_hbm,
    nv_hbm,
    op_hbm,
    x_ref,
    r_ref,
    res_v,
    nv_v,
    op_v,
    col_v,
    rows_v,
    cells,
    theta_buf,
    t_buf,
    zx_buf,
    local_sem,
    halo_send,
    halo_recv,
    sum_send,
    sum_recv,
    peers_in,
):
    nt, nz, nx = sizes
    t, z, x = lax.axis_index("ta"), lax.axis_index("gz"), lax.axis_index("gy")
    me_zx = z * nx + x
    loads = [
        pltpu.make_async_copy(nv_hbm, nv_v, local_sem.at[0]),
        pltpu.make_async_copy(res_hbm, res_v, local_sem.at[1]),
        pltpu.make_async_copy(op_hbm.at[t, 0, 0], op_v, local_sem.at[2]),
        pltpu.make_async_copy(op_hbm.at[:, 0, 0, 0], col_v, local_sem.at[3]),
    ]
    slots = [
        (3, (t, lax.rem(z + nz - 1, nz), x)),
        (4, (t, lax.rem(z + 1, nz), x)),
        (5, (t, z, lax.rem(x + nx - 1, nx))),
        (6, (t, z, lax.rem(x + 1, nx))),
        (1, (lax.rem(t + nt - 1, nt), z, x)),
        (2, (lax.rem(t + 1, nt), z, x)),
    ]
    my_t, my_zx = rank_of(t, nt), me_zx

    def t_peer(rank):
        return slab_of(rank, nt), z, x

    def zx_peer(rank):
        return t, lax.div(rank, nx), lax.rem(rank, nx)

    def signal_peers(semaphore, t_ranks, zx_ranks):
        for ranks, peer in ((t_ranks, t_peer), (zx_ranks, zx_peer)):
            def step(rank, carry, peer=peer):
                pl.semaphore_signal(semaphore, inc=1, device_id=peer(rank), device_id_type=MESH)
                return carry
            lax.fori_loop(*ranks, step, 0)

    barrier = pltpu.get_barrier_semaphore()
    for load in loads[:2]:
        load.start()
    for _, peer in slots:
        pl.semaphore_signal(barrier, inc=1, device_id=peer, device_id_type=MESH)
    for load in loads[2:]:
        load.start()
    signal_peers(barrier, (my_t + 1, nt), (my_zx + 1, nz * nx))
    t_peers = [t_peer(k) for k in others(nt, my_t)]
    zx_peers = [zx_peer(k) for k in others(nz * nx, my_zx)]

    loads[0].wait()
    loads[1].wait()
    start = restrict(nv_v, res_v, rows_v)
    pl.semaphore_wait(barrier, len(slots) + my_t + my_zx)

    def send_halo(k, field):
        own = packed(field)
        cells[k, 0] = own
        for m, peer in slots:
            pltpu.make_async_remote_copy(
                src_ref=cells.at[k, 0],
                dst_ref=cells.at[k, m],
                send_sem=halo_send.at[k],
                recv_sem=halo_recv.at[k],
                device_id=peer,
                device_id_type=MESH,
            ).start()
        cells[k, 7] = own
        cells[k, 8] = own

    def halo(k):
        return transfers(cells.at[k, pl.ds(1, 6)], slots[0][1], halo_send.at[k], halo_recv.at[k])

    def sums_of(k, buf, count, peer):
        return transfers(buf.at[pl.ds(0, count - 1)], peer, sum_send.at[k], sum_recv.at[k])

    send_halo(0, start)
    signal_peers(peers_in, (0, my_t), (0, my_zx))

    loads[3].wait()
    eye = lax.broadcasted_iota(jnp.int32, (CDOF, CDOF), 0) == lax.broadcasted_iota(jnp.int32, (CDOF, CDOF), 1)
    trace = [jnp.zeros((CDOF, CDOF), F32), jnp.zeros((CDOF, CDOF), F32)]
    square = jnp.zeros((CDOF, CDOF), F32)
    for slab in range(nt):
        for part in range(2):
            block = col_v[slab, part].astype(F32)
            trace[part] = trace[part] + block
            square = square + block * block
    scale = 1.0 / (nt * nz * nx * CDOF)
    stats = [jnp.where(eye, trace[0], 0.0), jnp.where(eye, trace[1], 0.0), square]
    stats = [jnp.sum(row_sum(value), axis=1, keepdims=True) * scale for value in stats]
    stats = jnp.concatenate([jnp.broadcast_to(value, (1, LANES)) for value in stats], axis=0)

    loads[2].wait()
    links = jnp.concatenate(
        [
            jnp.concatenate([op_v[m, part].astype(F32) for m in range(LINKS)], axis=1)
            for part in range(2)
        ],
        axis=0,
    ).astype(BF16)

    powers = [start]
    for k in range(3):
        halo(k).wait_recv()
        powers.append(apply_links(links, cells[k].reshape(LINKS * CDOF, LANES)))
        send_halo(k + 1, powers[k + 1])
        if k == 0:
            answers = nt - 1 - my_t + nz * nx - 1 - my_zx

            @pl.when(answers > 0)
            def _():
                pl.semaphore_wait(peers_in, answers)

            send_to_all(me_zx, zx_peers, stats, theta_buf, sum_send.at[0], sum_recv.at[0])

    sums_of(0, theta_buf, nz * nx, zx_peers[0]).wait_recv()
    stats = jnp.sum(theta_buf[...], axis=0)
    square = stats[2:3]
    inverse = jnp.where(square > 0.0, lax.rsqrt(jnp.where(square > 0.0, square, 1.0)), 1.0)
    theta = (stats[0:1] * inverse, stats[1:2] * inverse)
    weights = [inverse]
    for _ in range(3):
        weights.append(weights[-1] * inverse)

    def times_theta(field):
        return theta[0] * field + theta[1] * times_i(field)

    level = [start] + [powers[k] * weights[k - 1] for k in range(1, 4)]
    basis, last = [start], [times_theta(level[3])]
    for _ in range(3):
        level = [level[i + 1] - times_theta(level[i]) for i in range(len(level) - 1)]
        basis.append(level[0])
        last.append(times_theta(level[-1]))
    images = [basis[k + 1] + times_theta(basis[k]) for k in range(3)]
    turned = [times_i(image) for image in images]
    start_turned = times_i(start)

    pairs = [(i, j) for j in range(4) for i in range(j)]
    norms = [row_sum(images[k] * images[k]) for k in range(3)]
    right = [row_sum(images[k] * start) for k in range(3)]
    right_i = [row_sum(turned[k] * start) for k in range(3)]
    cross = [row_sum(images[i] * images[j]) for i, j in pairs[:3]]
    cross_i = [row_sum(turned[i] * images[j]) for i, j in pairs[:3]]

    halo(3).wait_recv()
    newest = apply_links(links, cells[3].reshape(LINKS * CDOF, LANES)) * weights[3]
    for part in last:
        newest = newest - part
    images.append(newest + last[3])
    norms.append(row_sum(images[3] * images[3]))
    right.append(row_sum(images[3] * start))
    right_i.append(-row_sum(images[3] * start_turned))
    cross += [row_sum(images[i] * images[3]) for i in range(3)]
    cross_i += [row_sum(turned[i] * images[3]) for i in range(3)]
    table = jnp.concatenate(norms + right + right_i + cross + cross_i, axis=0)
    table = table + pltpu.roll(table, 64, 1)
    table = jnp.where(lane_iota(table.shape) < NRHS, table, 0.0)
    dense = jnp.concatenate(
        [
            row_sum(pltpu.roll(table[8 * g : 8 * g + 8], 0, 1, stride=NRHS, stride_axis=0))
            for g in range(3)
        ],
        axis=0,
    )

    send_to_all(t, t_peers, dense, t_buf, sum_send.at[1], sum_recv.at[1])
    turned.append(times_i(images[3]))
    basis_turned = [times_i(field) for field in basis]
    sums_of(1, t_buf, nt, t_peers[0]).wait_recv()
    dense = jnp.sum(t_buf[...], axis=0)
    send_to_all(me_zx, zx_peers, dense, zx_buf, sum_send.at[2], sum_recv.at[2])
    sums_of(2, zx_buf, nz * nx, zx_peers[0]).wait_recv()
    dense = jnp.sum(zx_buf[...], axis=0)

    sums = []
    for g in range(3):
        spread = pltpu.roll(jnp.broadcast_to(dense[g : g + 1], (8, LANES)), 0, 1, stride=NRHS, stride_axis=0)
        sums += [spread[(8 - i) % 8 : (8 - i) % 8 + 1] for i in range(8)]
    diag = sums[0:4]
    right = [(sums[4 + k], sums[8 + k]) for k in range(4)]
    upper = {pair: (sums[12 + n], sums[18 + n]) for n, pair in enumerate(pairs)}
    coef = [(both_halves(c[0]), both_halves(c[1])) for c in solve(diag, upper, right)]

    field = None
    remain = start
    for k in range(4):
        cr, ci = coef[k]
        term = (cr * basis[k] + ci * basis_turned[k]) * inverse
        field = term if field is None else field + term
        remain = remain - cr * images[k] - ci * turned[k]
    x_ref[...] = field
    r_ref[...] = remain

    for k in range(4):
        halo(k).wait_send()
    sums_of(0, theta_buf, nz * nx, zx_peers[0]).wait_send()
    sums_of(1, t_buf, nt, t_peers[0]).wait_send()
    sums_of(2, zx_buf, nz * nx, zx_peers[0]).wait_send()


def prolong_kernel(x_ref, r_ref, nv_ref, out_ref, remain_ref, rows_v):
    x = x_ref[...].astype(BF16).astype(F32)
    upper, lower = x[:NVEC], x[NVEC:]
    every = upper + pltpu.roll(upper, NRHS, 1) + pltpu.roll(lower, 2 * NRHS, 1) + pltpu.roll(lower, 3 * NRHS, 1)
    every = jnp.concatenate([every, times_i(every)], axis=0)
    group = group_of(every.shape)
    for s in range(4):
        rows_v[pl.ds(s, 2 * NVEC, stride=4), :] = jnp.where(group == s, every, 0.0)
    weights = rows_v[...].T.astype(BF16)
    for colour in range(3):
        basis = nv_ref[:, :, colour].reshape(2 * NVEC * 4, 512)
        value = jnp.dot(weights, basis, preferred_element_type=F32)
        out_ref[:, :, colour] = value.astype(BF16).reshape(2, 4, NRHS, 512)
    turned = r_ref[...].T
    remain_ref[0] = turned[0:NRHS]
    remain_ref[1] = turned[64 : 64 + NRHS]


def body(sizes, residual, null_vectors, coarse_op):
    sites = residual.shape[-1]
    res = residual.reshape(2, 4, 3, NRHS, sites)
    nv = null_vectors.transpose(0, 1, 3, 4, 5, 6, 2, 7).reshape(2, NVEC, 3, 4, sites)
    nt, nz, nx = sizes
    any_spec = pl.BlockSpec(memory_space=pltpu.HBM)
    vmem_spec = pl.BlockSpec(memory_space=pltpu.VMEM)
    field = jax.ShapeDtypeStruct((CDOF, LANES), F32)
    far = [pltpu.with_memory_space_constraint(a, pltpu.HBM) for a in (res, nv, coarse_op)]
    x, r = pl.pallas_call(
        functools.partial(coarse_kernel, sizes),
        out_shape=(field, field),
        in_specs=[any_spec] * 3,
        out_specs=(vmem_spec, vmem_spec),
        scratch_shapes=[
            pltpu.VMEM(res.shape, BF16),
            pltpu.VMEM(nv.shape, BF16),
            pltpu.VMEM((LINKS, 2, CDOF, CDOF), BF16),
            pltpu.VMEM((nt, 2, CDOF, CDOF), BF16),
            pltpu.VMEM((2 * NVEC * 4, LANES), F32),
            pltpu.VMEM((4, LINKS, CDOF, LANES), BF16),
            pltpu.VMEM((nz * nx, 3, LANES), F32),
            pltpu.VMEM((nt, 3, LANES), F32),
            pltpu.VMEM((nz * nx, 3, LANES), F32),
            pltpu.SemaphoreType.DMA((4,)),
            pltpu.SemaphoreType.DMA((4,)),
            pltpu.SemaphoreType.DMA((4,)),
            pltpu.SemaphoreType.DMA((3,)),
            pltpu.SemaphoreType.DMA((3,)),
            pltpu.SemaphoreType.REGULAR,
        ],
        compiler_params=pltpu.CompilerParams(
            collective_id=0, has_side_effects=True, vmem_limit_bytes=16 * 1024 * 1024
        ),
    )(*far)
    correction, remain = pl.pallas_call(
        prolong_kernel,
        out_shape=(
            jax.ShapeDtypeStruct((2, 4, 3, NRHS, sites), BF16),
            jax.ShapeDtypeStruct((2, NRHS, CDOF), F32),
        ),
        in_specs=[vmem_spec] * 3,
        out_specs=(vmem_spec, vmem_spec),
        scratch_shapes=[pltpu.VMEM((2 * NVEC * 4, LANES), F32)],
        compiler_params=pltpu.CompilerParams(vmem_limit_bytes=16 * 1024 * 1024),
    )(x, r, nv)
    correction = correction.reshape(2, 4, 3, NRHS, 1, 1, 1, sites)
    remain = remain.transpose(0, 2, 1).reshape(2, CDOF, 1, 1, 1, NRHS)
    return correction, remain


def solution(mesh):
    sizes = (mesh.shape["ta"], mesh.shape["gz"], mesh.shape["gy"])
    return jax.shard_map(
        functools.partial(body, sizes),
        mesh=mesh,
        in_specs=(
            P(None, None, None, None, "ta", "gz", "gy", None),
            P(None, None, None, None, "ta", "gz", "gy", None),
            P(None, "gz", "gy", None, None, None, None),
        ),
        out_specs=(
            P(None, None, None, None, "ta", "gz", "gy", None),
            P(None, None, "ta", "gz", "gy", None),
        ),
        check_vma=False,
    )
```

```python
import functools

import jax
import jax.numpy as jnp
from jax import lax
from jax.experimental import pallas as pl
from jax.experimental.pallas import tpu as pltpu
from jax.sharding import PartitionSpec as P

MESH = pl.DeviceIdType.MESH
F32 = jnp.float32
BF16 = jnp.bfloat16
CDOF = 48
NVEC = 24
NRHS = 16
LINKS = 9
LANES = 128


def lane_iota(shape):
    return lax.broadcasted_iota(jnp.int32, shape, len(shape) - 1)


def group_of(shape):
    return lax.rem(lax.div(lane_iota(shape), NRHS), 4)


def sign_of(shape):
    return jnp.where(lane_iota(shape) < 64, -1.0, 1.0).astype(F32)


def times_i(field):
    return sign_of(field.shape) * pltpu.roll(field, 64, 1)


def restrict(loads, nv_ref, res_ref, basis_ref, rows_ref):
    total = None
    for colour in range(3):
        for load in loads[colour]:
            load.wait()
        basis = nv_ref[colour].reshape(2 * NVEC * 4, 512)
        basis_ref[colour] = basis
        source = res_ref[colour].reshape(2 * 4 * NRHS, 512)
        part = lax.dot_general(basis, source, (((1,), (1,)), ((), ())), preferred_element_type=F32)
        total = part if total is None else total + part
    rows_ref[...] = total
    by_spin = [rows_ref[pl.ds(s, 2 * NVEC, stride=4), :] for s in range(4)]
    group = group_of((2 * NVEC, LANES))
    halves = []
    for chirality in range(2):
        a, b = 2 * chirality, 2 * chirality + 1
        picked = jnp.where(group == a, by_spin[a], jnp.where(group == b, by_spin[b], 0.0))
        picked = picked + pltpu.roll(picked, LANES - NRHS, 1)
        if chirality == 1:
            picked = pltpu.roll(picked, LANES - 2 * NRHS, 1)
        halves.append(picked[:NVEC] - times_i(picked[NVEC:]))
    field = jnp.concatenate(halves, axis=0)
    return jnp.where(group == 0, field, 0.0)


def split(wide):
    group = group_of(wide.shape)
    high = wide.astype(BF16).astype(F32)
    return jnp.where(group == 0, high, jnp.where(group == 2, wide - high, 0.0)).astype(BF16)


def both_groups(field):
    return field + pltpu.roll(field, 2 * NRHS, 1)


def combine(product):
    real, imag = product[:CDOF], product[CDOF:]
    first = group_of(real.shape) == 0
    back, forth = LANES - 2 * NRHS, 2 * NRHS
    total = real + jnp.where(first, pltpu.roll(real, back, 1), pltpu.roll(real, forth, 1))
    cross = pltpu.roll(imag, 64, 1) + jnp.where(first, pltpu.roll(imag, forth, 1), pltpu.roll(imag, back, 1))
    return total + sign_of(real.shape) * cross


def first_group(wide):
    return jnp.where(group_of(wide.shape) == 0, wide, 0.0)


def row_sum(product):
    return jnp.sum(product, axis=0, keepdims=True)


def cmul(a, b):
    return a[0] * b[0] - a[1] * b[1], a[0] * b[1] + a[1] * b[0]


def cmul_conj(a, b):
    return a[0] * b[0] + a[1] * b[1], a[0] * b[1] - a[1] * b[0]


def csub(a, b):
    return a[0] - b[0], a[1] - b[1]


def solve(diag, upper, right):
    n = len(diag)
    d, inv, low = [], [], {}
    for j in range(n):
        value = diag[j]
        for k in range(j):
            value = value - d[k] * (low[j, k][0] ** 2 + low[j, k][1] ** 2)
        d.append(value)
        inv.append(1.0 / value)
        for i in range(j + 1, n):
            entry = (upper[j, i][0], -upper[j, i][1])
            for k in range(j):
                term = cmul_conj(low[j, k], low[i, k])
                entry = csub(entry, (d[k] * term[0], d[k] * term[1]))
            low[i, j] = (entry[0] * inv[j], entry[1] * inv[j])
    y = []
    for i in range(n):
        value = right[i]
        for k in range(i):
            value = csub(value, cmul(low[i, k], y[k]))
        y.append(value)
    c = [None] * n
    for i in reversed(range(n)):
        value = (y[i][0] * inv[i], y[i][1] * inv[i])
        for k in range(i + 1, n):
            value = csub(value, cmul_conj(low[k, i], c[k]))
        c[i] = value
    return c


def both_halves(row):
    row = jnp.where(lane_iota(row.shape) < NRHS, row, 0.0)
    return row + pltpu.roll(row, 64, 1)


def others(count, me):
    return [k + jnp.where(k >= me, 1, 0) for k in range(count - 1)]


def rank_of(t, nt):
    half = nt // 2
    y = lax.div(t, 2)
    r = jnp.where(y == 0, 0, jnp.where(y <= half // 2, 2 * y - 1, 2 * (half - y)))
    return 2 * r + lax.rem(t, 2)


def slab_of(rank, nt):
    half = nt // 2
    r = lax.div(rank, 2)
    y = jnp.where(lax.rem(r, 2) == 1, lax.div(r + 1, 2), lax.rem(half - lax.div(r, 2), half))
    return 2 * y + lax.rem(rank, 2)


def send_to_all(me, peers, value, buf, send_sem, recv_sem):
    buf[me] = value
    for peer in peers:
        pltpu.make_async_remote_copy(
            src_ref=buf.at[me],
            dst_ref=buf.at[me],
            send_sem=send_sem,
            recv_sem=recv_sem,
            device_id=peer,
            device_id_type=MESH,
        ).start()


def transfers(block, peer, send_sem, recv_sem):
    return pltpu.make_async_remote_copy(
        src_ref=block, dst_ref=block, send_sem=send_sem, recv_sem=recv_sem, device_id=peer, device_id_type=MESH
    )


def coarse_kernel(
    sizes,
    res_hbm,
    nv_hbm,
    op_hbm,
    x_ref,
    r_ref,
    basis_ref,
    res_v,
    nv_v,
    op_v,
    col_v,
    rows_v,
    cells,
    theta_buf,
    t_buf,
    zx_buf,
    local_sem,
    halo_send,
    near_recv,
    halo_recv,
    sum_send,
    sum_recv,
    peers_in,
):
    nt, nz, nx = sizes
    t, z, x = lax.axis_index("ta"), lax.axis_index("gz"), lax.axis_index("gy")
    me_zx = z * nx + x
    loads = [
        (
            pltpu.make_async_copy(nv_hbm.at[:, :, colour], nv_v.at[colour], local_sem.at[2 * colour]),
            pltpu.make_async_copy(res_hbm.at[:, :, colour], res_v.at[colour], local_sem.at[2 * colour + 1]),
        )
        for colour in range(3)
    ]
    op_load = pltpu.make_async_copy(op_hbm.at[t, 0, 0], op_v, local_sem.at[6])
    col_load = pltpu.make_async_copy(op_hbm.at[:, 0, 0, 0], col_v, local_sem.at[7])
    slots = [
        (5, (t, lax.rem(z + nz - 1, nz), x)),
        (6, (t, lax.rem(z + 1, nz), x)),
        (7, (t, z, lax.rem(x + nx - 1, nx))),
        (8, (t, z, lax.rem(x + 1, nx))),
        (3, (lax.rem(t + nt - 1, nt), z, x)),
        (4, (lax.rem(t + 1, nt), z, x)),
    ]
    my_t, my_zx = rank_of(t, nt), me_zx

    def t_peer(rank):
        return slab_of(rank, nt), z, x

    def zx_peer(rank):
        return t, lax.div(rank, nx), lax.rem(rank, nx)

    def signal_peers(semaphore, t_ranks, zx_ranks):
        for ranks, peer in ((t_ranks, t_peer), (zx_ranks, zx_peer)):
            def step(rank, carry, peer=peer):
                pl.semaphore_signal(semaphore, inc=1, device_id=peer(rank), device_id_type=MESH)
                return carry
            lax.fori_loop(*ranks, step, 0)

    barrier = pltpu.get_barrier_semaphore()
    for pair in loads:
        for load in pair:
            load.start()
    for _, peer in slots:
        pl.semaphore_signal(barrier, inc=1, device_id=peer, device_id_type=MESH)
    signal_peers(barrier, (my_t + 1, nt), (my_zx + 1, nz * nx))
    t_peers = [t_peer(k) for k in others(nt, my_t)]
    zx_peers = [zx_peer(k) for k in others(nz * nx, my_zx)]

    op_load.start()
    col_load.start()
    start = restrict(loads, nv_v, res_v, basis_ref, rows_v)
    pl.semaphore_wait(barrier, len(slots) + my_t + my_zx)

    def send_halo(k, wide):
        own = split(wide)
        cells[k, 0] = own
        for m, peer in slots:
            pltpu.make_async_remote_copy(
                src_ref=cells.at[k, 0],
                dst_ref=cells.at[k, m],
                send_sem=halo_send.at[k],
                recv_sem=(near_recv if m < 5 else halo_recv).at[k],
                device_id=peer,
                device_id_type=MESH,
            ).start()
        cells[k, 1] = own
        cells[k, 2] = own

    def apply_links(k):
        transfers(cells.at[k, pl.ds(3, 2)], slots[0][1], halo_send.at[k], near_recv.at[k]).wait_recv()
        near = jnp.dot(links[0], cells[k, 0:5].reshape(5 * CDOF, LANES), preferred_element_type=F32)
        transfers(cells.at[k, pl.ds(5, 4)], slots[0][1], halo_send.at[k], halo_recv.at[k]).wait_recv()
        far = jnp.dot(links[1], cells[k, 5:9].reshape(4 * CDOF, LANES), preferred_element_type=F32)
        return combine(near + far)

    def sums_of(k, buf, count, peer):
        return transfers(buf.at[pl.ds(0, count - 1)], peer, sum_send.at[k], sum_recv.at[k])

    send_halo(0, both_groups(start))
    signal_peers(peers_in, (0, my_t), (0, my_zx))

    col_load.wait()
    eye = lax.broadcasted_iota(jnp.int32, (CDOF, CDOF), 0) == lax.broadcasted_iota(jnp.int32, (CDOF, CDOF), 1)
    trace = [jnp.zeros((CDOF, CDOF), F32), jnp.zeros((CDOF, CDOF), F32)]
    square = jnp.zeros((CDOF, CDOF), F32)
    for slab in range(nt):
        for part in range(2):
            block = col_v[slab, part].astype(F32)
            trace[part] = trace[part] + block
            square = square + block * block
    scale = 1.0 / (nt * nz * nx * CDOF)
    stats = [jnp.where(eye, trace[0], 0.0), jnp.where(eye, trace[1], 0.0), square]
    stats = [jnp.sum(row_sum(value), axis=1, keepdims=True) * scale for value in stats]
    stats = jnp.concatenate([jnp.broadcast_to(value, (1, LANES)) for value in stats], axis=0)

    op_load.wait()
    links = [
        jnp.concatenate(
            [jnp.concatenate([op_v[m, part].astype(F32) for m in order], axis=1) for part in range(2)], axis=0
        ).astype(BF16)
        for order in ((0, 7, 8, 1, 2), (3, 4, 5, 6))
    ]

    powers = [start]
    for k in range(3):
        wide = apply_links(k)
        send_halo(k + 1, wide)
        powers.append(first_group(wide))
        if k == 0:
            answers = nt - 1 - my_t + nz * nx - 1 - my_zx

            @pl.when(answers > 0)
            def _():
                pl.semaphore_wait(peers_in, answers)

            send_to_all(me_zx, zx_peers, stats, theta_buf, sum_send.at[0], sum_recv.at[0])

    sums_of(0, theta_buf, nz * nx, zx_peers[0]).wait_recv()
    stats = jnp.sum(theta_buf[...], axis=0)
    square = stats[2:3]
    inverse = jnp.where(square > 0.0, lax.rsqrt(jnp.where(square > 0.0, square, 1.0)), 1.0)
    theta = (stats[0:1] * inverse, stats[1:2] * inverse)
    weights = [inverse]
    for _ in range(3):
        weights.append(weights[-1] * inverse)

    def times_theta(field):
        return theta[0] * field + theta[1] * times_i(field)

    level = [start] + [powers[k] * weights[k - 1] for k in range(1, 4)]
    basis, last = [start], [times_theta(level[3])]
    for _ in range(3):
        level = [level[i + 1] - times_theta(level[i]) for i in range(len(level) - 1)]
        basis.append(level[0])
        last.append(times_theta(level[-1]))
    images = [basis[k + 1] + times_theta(basis[k]) for k in range(3)]
    turned = [times_i(image) for image in images]
    start_turned = times_i(start)

    def row_of(rows, first):
        table = jnp.concatenate(rows, axis=0)
        table = table + pltpu.roll(table, 64, 1)
        table = jnp.where(lane_iota(table.shape) < NRHS, table, 0.0)
        return row_sum(pltpu.roll(table, first * NRHS, 1, stride=NRHS, stride_axis=0))

    early_pairs, late_pairs = [(0, 1), (0, 2), (1, 2)], [(0, 3), (1, 3), (2, 3)]
    early = [row_sum(images[k] * images[k]) for k in range(3)]
    early += [row_sum(images[k] * start) for k in range(3)]
    early += [row_sum(turned[k] * start) for k in range(3)]
    early += [row_sum(images[i] * images[j]) for i, j in early_pairs]
    early += [row_sum(turned[i] * images[j]) for i, j in early_pairs]
    early = [row_of(early[:8], 0), row_of(early[8:15] + [jnp.zeros((1, LANES), F32)], 0)]

    newest = first_group(apply_links(3)) * weights[3]
    for part in last:
        newest = newest - part
    images.append(newest + last[3])
    late = [row_sum(images[3] * images[3]), row_sum(images[3] * start), -row_sum(images[3] * start_turned)]
    late += [row_sum(images[i] * images[3]) for i in range(3)]
    late += [row_sum(turned[i] * images[3]) for i in range(3)]
    seven = jnp.concatenate([late[0], jnp.zeros((7, LANES), F32)], axis=0)
    seven = seven + pltpu.roll(seven, 64, 1)
    seven = pltpu.roll(jnp.where(lane_iota(seven.shape) < NRHS, seven, 0.0), 7 * NRHS, 1)[0:1]
    dense = jnp.concatenate([early[0], early[1] + seven, row_of(late[1:], 0)], axis=0)

    send_to_all(t, t_peers, dense, t_buf, sum_send.at[1], sum_recv.at[1])
    turned.append(times_i(images[3]))
    basis_turned = [times_i(field) for field in basis]
    sums_of(1, t_buf, nt, t_peers[0]).wait_recv()
    dense = jnp.sum(t_buf[...], axis=0)
    send_to_all(me_zx, zx_peers, dense, zx_buf, sum_send.at[2], sum_recv.at[2])
    sums_of(2, zx_buf, nz * nx, zx_peers[0]).wait_recv()
    dense = jnp.sum(zx_buf[...], axis=0)

    sums = []
    for g in range(3):
        spread = pltpu.roll(jnp.broadcast_to(dense[g : g + 1], (8, LANES)), 0, 1, stride=NRHS, stride_axis=0)
        sums += [spread[(8 - i) % 8 : (8 - i) % 8 + 1] for i in range(8)]
    diag = sums[0:3] + [sums[15]]
    right = [(sums[3 + k], sums[6 + k]) for k in range(3)] + [(sums[16], sums[17])]
    upper = {pair: (sums[9 + n], sums[12 + n]) for n, pair in enumerate(early_pairs)}
    upper.update({pair: (sums[18 + n], sums[21 + n]) for n, pair in enumerate(late_pairs)})
    coef = [(both_halves(c[0]), both_halves(c[1])) for c in solve(diag, upper, right)]

    field = None
    remain = start
    for k in range(4):
        cr, ci = coef[k]
        term = (cr * basis[k] + ci * basis_turned[k]) * inverse
        field = term if field is None else field + term
        remain = remain - cr * images[k] - ci * turned[k]
    x_ref[...] = field
    r_ref[...] = remain

    for k in range(4):
        transfers(cells.at[k, pl.ds(3, 6)], slots[0][1], halo_send.at[k], halo_recv.at[k]).wait_send()
    sums_of(0, theta_buf, nz * nx, zx_peers[0]).wait_send()
    sums_of(1, t_buf, nt, t_peers[0]).wait_send()
    sums_of(2, zx_buf, nz * nx, zx_peers[0]).wait_send()


def prolong_kernel(x_ref, r_ref, basis_ref, out_ref, remain_ref, rows_v):
    x = x_ref[...].astype(BF16).astype(F32)
    upper, lower = x[:NVEC], x[NVEC:]
    every = upper + pltpu.roll(upper, NRHS, 1) + pltpu.roll(lower, 2 * NRHS, 1) + pltpu.roll(lower, 3 * NRHS, 1)
    every = jnp.concatenate([every, times_i(every)], axis=0)
    group = group_of(every.shape)
    for s in range(4):
        rows_v[pl.ds(s, 2 * NVEC, stride=4), :] = jnp.where(group == s, every, 0.0)
    weights = rows_v[...].T.astype(BF16)
    for colour in range(3):
        value = jnp.dot(weights, basis_ref[colour], preferred_element_type=F32)
        out_ref[:, :, colour] = value.astype(BF16).reshape(2, 4, NRHS, 512)
    turned = r_ref[...].T
    remain_ref[0] = turned[0:NRHS]
    remain_ref[1] = turned[64 : 64 + NRHS]


def body(sizes, residual, null_vectors, coarse_op):
    sites = residual.shape[-1]
    res = residual.reshape(2, 4, 3, NRHS, sites)
    nv = null_vectors.transpose(0, 1, 3, 4, 5, 6, 2, 7).reshape(2, NVEC, 3, 4, sites)
    nt, nz, nx = sizes
    any_spec = pl.BlockSpec(memory_space=pltpu.HBM)
    vmem_spec = pl.BlockSpec(memory_space=pltpu.VMEM)
    field = jax.ShapeDtypeStruct((CDOF, LANES), F32)
    far = [pltpu.with_memory_space_constraint(a, pltpu.HBM) for a in (res, nv, coarse_op)]
    x, r, basis = pl.pallas_call(
        functools.partial(coarse_kernel, sizes),
        out_shape=(field, field, jax.ShapeDtypeStruct((3, 2 * NVEC * 4, sites), BF16)),
        in_specs=[any_spec] * 3,
        out_specs=(vmem_spec,) * 3,
        scratch_shapes=[
            pltpu.VMEM((3, 2, 4, NRHS, sites), BF16),
            pltpu.VMEM((3, 2, NVEC, 4, sites), BF16),
            pltpu.VMEM((LINKS, 2, CDOF, CDOF), BF16),
            pltpu.VMEM((nt, 2, CDOF, CDOF), BF16),
            pltpu.VMEM((2 * NVEC * 4, LANES), F32),
            pltpu.VMEM((4, LINKS, CDOF, LANES), BF16),
            pltpu.VMEM((nz * nx, 3, LANES), F32),
            pltpu.VMEM((nt, 3, LANES), F32),
            pltpu.VMEM((nz * nx, 3, LANES), F32),
            pltpu.SemaphoreType.DMA((8,)),
            pltpu.SemaphoreType.DMA((4,)),
            pltpu.SemaphoreType.DMA((4,)),
            pltpu.SemaphoreType.DMA((4,)),
            pltpu.SemaphoreType.DMA((3,)),
            pltpu.SemaphoreType.DMA((3,)),
            pltpu.SemaphoreType.REGULAR,
        ],
        compiler_params=pltpu.CompilerParams(
            collective_id=0, has_side_effects=True, vmem_limit_bytes=16 * 1024 * 1024
        ),
    )(*far)
    correction, remain = pl.pallas_call(
        prolong_kernel,
        out_shape=(
            jax.ShapeDtypeStruct((2, 4, 3, NRHS, sites), BF16),
            jax.ShapeDtypeStruct((2, NRHS, CDOF), F32),
        ),
        in_specs=[vmem_spec] * 3,
        out_specs=(vmem_spec, vmem_spec),
        scratch_shapes=[pltpu.VMEM((2 * NVEC * 4, LANES), F32)],
        compiler_params=pltpu.CompilerParams(vmem_limit_bytes=16 * 1024 * 1024),
    )(x, r, basis)
    correction = correction.reshape(2, 4, 3, NRHS, 1, 1, 1, sites)
    remain = remain.transpose(0, 2, 1).reshape(2, CDOF, 1, 1, 1, NRHS)
    return correction, remain


def solution(mesh):
    sizes = (mesh.shape["ta"], mesh.shape["gz"], mesh.shape["gy"])
    return jax.shard_map(
        functools.partial(body, sizes),
        mesh=mesh,
        in_specs=(
            P(None, None, None, None, "ta", "gz", "gy", None),
            P(None, None, None, None, "ta", "gz", "gy", None),
            P(None, "gz", "gy", None, None, None, None),
        ),
        out_specs=(
            P(None, None, None, None, "ta", "gz", "gy", None),
            P(None, None, "ta", "gz", "gy", None),
        ),
        check_vma=False,
    )
```

```python
import functools

import jax
import jax.numpy as jnp
from jax import lax
from jax.experimental import pallas as pl
from jax.experimental.pallas import tpu as pltpu
from jax.sharding import PartitionSpec as P

MESH = pl.DeviceIdType.MESH
F32 = jnp.float32
BF16 = jnp.bfloat16
CDOF = 48
NVEC = 24
NRHS = 16
LINKS = 9
LANES = 128


def lane_iota(shape):
    return lax.broadcasted_iota(jnp.int32, shape, len(shape) - 1)


def group_of(shape):
    return lax.rem(lax.div(lane_iota(shape), NRHS), 4)


def sign_of(shape):
    return jnp.where(lane_iota(shape) < 64, -1.0, 1.0).astype(F32)


def times_i(field):
    return sign_of(field.shape) * pltpu.roll(field, 64, 1)


def restrict(loads, nv_ref, res_ref, basis_ref, rows_ref):
    total = None
    for colour in range(3):
        for load in loads[colour]:
            load.wait()
        basis = nv_ref[colour].reshape(2 * NVEC * 4, 512)
        basis_ref[colour] = basis
        source = res_ref[colour].reshape(2 * 4 * NRHS, 512)
        part = lax.dot_general(basis, source, (((1,), (1,)), ((), ())), preferred_element_type=F32)
        total = part if total is None else total + part
    rows_ref[...] = total
    by_spin = [rows_ref[pl.ds(s, 2 * NVEC, stride=4), :] for s in range(4)]
    group = group_of((2 * NVEC, LANES))
    halves = []
    for chirality in range(2):
        a, b = 2 * chirality, 2 * chirality + 1
        picked = jnp.where(group == a, by_spin[a], jnp.where(group == b, by_spin[b], 0.0))
        picked = picked + pltpu.roll(picked, LANES - NRHS, 1)
        if chirality == 1:
            picked = pltpu.roll(picked, LANES - 2 * NRHS, 1)
        halves.append(picked[:NVEC] - times_i(picked[NVEC:]))
    field = jnp.concatenate(halves, axis=0)
    return jnp.where(group == 0, field, 0.0)


def split(wide):
    group = group_of(wide.shape)
    high = wide.astype(BF16).astype(F32)
    return jnp.where(group == 0, high, jnp.where(group == 2, wide - high, 0.0)).astype(BF16)


def both_groups(field):
    return field + pltpu.roll(field, 2 * NRHS, 1)


def combine(product):
    real, imag = product[:CDOF], product[CDOF:]
    first = group_of(real.shape) == 0
    back, forth = LANES - 2 * NRHS, 2 * NRHS
    total = real + jnp.where(first, pltpu.roll(real, back, 1), pltpu.roll(real, forth, 1))
    cross = pltpu.roll(imag, 64, 1) + jnp.where(first, pltpu.roll(imag, forth, 1), pltpu.roll(imag, back, 1))
    return total + sign_of(real.shape) * cross


def first_group(wide):
    return jnp.where(group_of(wide.shape) == 0, wide, 0.0)


def row_sum(product):
    return jnp.sum(product, axis=0, keepdims=True)


def cmul(a, b):
    return a[0] * b[0] - a[1] * b[1], a[0] * b[1] + a[1] * b[0]


def cmul_conj(a, b):
    return a[0] * b[0] + a[1] * b[1], a[0] * b[1] - a[1] * b[0]


def csub(a, b):
    return a[0] - b[0], a[1] - b[1]


def solve(diag, upper, right):
    n = len(diag)
    d, inv, low = [], [], {}
    for j in range(n):
        value = diag[j]
        for k in range(j):
            value = value - d[k] * (low[j, k][0] ** 2 + low[j, k][1] ** 2)
        d.append(value)
        inv.append(1.0 / value)
        for i in range(j + 1, n):
            entry = (upper[j, i][0], -upper[j, i][1])
            for k in range(j):
                term = cmul_conj(low[j, k], low[i, k])
                entry = csub(entry, (d[k] * term[0], d[k] * term[1]))
            low[i, j] = (entry[0] * inv[j], entry[1] * inv[j])
    y = []
    for i in range(n):
        value = right[i]
        for k in range(i):
            value = csub(value, cmul(low[i, k], y[k]))
        y.append(value)
    c = [None] * n
    for i in reversed(range(n)):
        value = (y[i][0] * inv[i], y[i][1] * inv[i])
        for k in range(i + 1, n):
            value = csub(value, cmul_conj(low[k, i], c[k]))
        c[i] = value
    return c


def both_halves(row):
    row = jnp.where(lane_iota(row.shape) < NRHS, row, 0.0)
    return row + pltpu.roll(row, 64, 1)


def others(count, me):
    return [k + jnp.where(k >= me, 1, 0) for k in range(count - 1)]


def rank_of(t, nt):
    half = nt // 2
    y = lax.div(t, 2)
    r = jnp.where(y == 0, 0, jnp.where(y <= half // 2, 2 * y - 1, 2 * (half - y)))
    return 2 * r + lax.rem(t, 2)


def slab_of(rank, nt):
    half = nt // 2
    r = lax.div(rank, 2)
    y = jnp.where(lax.rem(r, 2) == 1, lax.div(r + 1, 2), lax.rem(half - lax.div(r, 2), half))
    return 2 * y + lax.rem(rank, 2)


def ball(sizes):
    steps = [(1, 0, 0), (-1, 0, 0), (0, 1, 0), (0, -1, 0), (0, 0, 1), (0, 0, -1)]
    found = [(0, 0, 0)] + [shifted((0, 0, 0), step, sizes) for step in steps]
    for a in steps:
        for b in steps:
            site = shifted(shifted((0, 0, 0), a, sizes), b, sizes)
            if site not in found:
                found.append(site)
    return steps, found


def shifted(site, step, sizes):
    return tuple((a + b) % n for a, b, n in zip(site, step, sizes))


def pack_links(op_ref):
    def rows(part):
        near = [op_ref[m, part].astype(F32) for m in (0, 7, 8, 1, 2)]
        far = [op_ref[m, part].astype(F32) for m in (3, 4, 5, 6)]
        return jnp.concatenate(near + [jnp.zeros((CDOF, 16), F32)] + far + [jnp.zeros((CDOF, 64), F32)], axis=1)

    return jnp.concatenate([rows(0), rows(1)], axis=0).astype(BF16)


def times_links(links, near, far):
    value = jnp.dot(links[:, : 5 * CDOF], near, preferred_element_type=F32)
    return combine(value + jnp.dot(links[:, 256 : 256 + 4 * CDOF], far, preferred_element_type=F32))


def send_to_all(me, peers, value, buf, send_sem, recv_sem):
    buf[me] = value
    for peer in peers:
        pltpu.make_async_remote_copy(
            src_ref=buf.at[me],
            dst_ref=buf.at[me],
            send_sem=send_sem,
            recv_sem=recv_sem,
            device_id=peer,
            device_id_type=MESH,
        ).start()


def transfers(block, peer, send_sem, recv_sem):
    return pltpu.make_async_remote_copy(
        src_ref=block, dst_ref=block, send_sem=send_sem, recv_sem=recv_sem, device_id=peer, device_id_type=MESH
    )


def coarse_kernel(
    sizes,
    res_hbm,
    nv_hbm,
    op_hbm,
    x_ref,
    r_ref,
    basis_ref,
    res_v,
    nv_v,
    op_v,
    col_v,
    rows_v,
    cells,
    links_v,
    ball_v,
    theta_buf,
    t_buf,
    zx_buf,
    local_sem,
    halo_send,
    near_recv,
    halo_recv,
    sum_send,
    sum_recv,
    peers_in,
    links_send,
    links_recv,
    ball_send,
    ball_recv,
):
    nt, nz, nx = sizes
    t, z, x = lax.axis_index("ta"), lax.axis_index("gz"), lax.axis_index("gy")
    me_zx = z * nx + x
    loads = [
        (
            pltpu.make_async_copy(nv_hbm.at[:, :, colour], nv_v.at[colour], local_sem.at[2 * colour]),
            pltpu.make_async_copy(res_hbm.at[:, :, colour], res_v.at[colour], local_sem.at[2 * colour + 1]),
        )
        for colour in range(3)
    ]
    op_loads = [
        pltpu.make_async_copy(op_hbm.at[slab, 0, 0], op_v.at[i], local_sem.at[6 + i])
        for i, slab in enumerate((t, lax.rem(t + 1, nt), lax.rem(t + nt - 1, nt)))
    ]
    col_load = pltpu.make_async_copy(op_hbm.at[:, 0, 0, 0], col_v, local_sem.at[9])
    steps, sites = ball(sizes)
    ball_peers = [
        (lax.rem(t + nt - a, nt), lax.rem(z + nz - b, nz), lax.rem(x + nx - c, nx)) for a, b, c in sites
    ]
    slots = [
        (5, (t, lax.rem(z + nz - 1, nz), x)),
        (6, (t, lax.rem(z + 1, nz), x)),
        (7, (t, z, lax.rem(x + nx - 1, nx))),
        (8, (t, z, lax.rem(x + 1, nx))),
        (3, (lax.rem(t + nt - 1, nt), z, x)),
        (4, (lax.rem(t + 1, nt), z, x)),
    ]
    my_t, my_zx = rank_of(t, nt), me_zx

    def t_peer(rank):
        return slab_of(rank, nt), z, x

    def zx_peer(rank):
        return t, lax.div(rank, nx), lax.rem(rank, nx)

    def signal_peers(semaphore, t_ranks, zx_ranks):
        for ranks, peer in ((t_ranks, t_peer), (zx_ranks, zx_peer)):
            def step(rank, carry, peer=peer):
                pl.semaphore_signal(semaphore, inc=1, device_id=peer(rank), device_id_type=MESH)
                return carry
            lax.fori_loop(*ranks, step, 0)

    barrier = pltpu.get_barrier_semaphore()
    for pair in loads:
        for load in pair:
            load.start()
    for peer in ball_peers[1:]:
        pl.semaphore_signal(barrier, inc=1, device_id=peer, device_id_type=MESH)
    signal_peers(barrier, (my_t + 1, nt), (my_zx + 1, nz * nx))
    t_peers = [t_peer(k) for k in others(nt, my_t)]
    zx_peers = [zx_peer(k) for k in others(nz * nx, my_zx)]

    for load in op_loads:
        load.start()
    col_load.start()
    start = restrict(loads, nv_v, res_v, basis_ref, rows_v)
    pl.semaphore_wait(barrier, len(sites) - 1 + my_t + my_zx)

    def send_halo(k, wide):
        own = split(wide)
        cells[k, 0] = own
        for m, peer in slots:
            pltpu.make_async_remote_copy(
                src_ref=cells.at[k, 0],
                dst_ref=cells.at[k, m],
                send_sem=halo_send.at[k],
                recv_sem=(near_recv if m < 5 else halo_recv).at[k],
                device_id=peer,
                device_id_type=MESH,
            ).start()
        cells[k, 1] = own
        cells[k, 2] = own

    def apply_links(k):
        transfers(cells.at[k, pl.ds(3, 2)], slots[0][1], halo_send.at[k], near_recv.at[k]).wait_recv()
        near = jnp.dot(
            links_v[0, :, : 5 * CDOF], cells[k, 0:5].reshape(5 * CDOF, LANES), preferred_element_type=F32
        )
        transfers(cells.at[k, pl.ds(5, 4)], slots[0][1], halo_send.at[k], halo_recv.at[k]).wait_recv()
        far = jnp.dot(
            links_v[0, :, 256 : 256 + 4 * CDOF], cells[k, 5:9].reshape(4 * CDOF, LANES), preferred_element_type=F32
        )
        return combine(near + far)

    def sums_of(k, buf, count, peer):
        return transfers(buf.at[pl.ds(0, count - 1)], peer, sum_send.at[k], sum_recv.at[k])

    send_halo(0, both_groups(start))
    signal_peers(peers_in, (0, my_t), (0, my_zx))

    op_loads[0].wait()
    links_v[0] = pack_links(op_v.at[0])
    for i in range(3, 7):
        pltpu.make_async_remote_copy(
            src_ref=links_v.at[0],
            dst_ref=links_v.at[i],
            send_sem=links_send,
            recv_sem=links_recv,
            device_id=ball_peers[i],
            device_id_type=MESH,
        ).start()

    col_load.wait()
    eye = lax.broadcasted_iota(jnp.int32, (CDOF, CDOF), 0) == lax.broadcasted_iota(jnp.int32, (CDOF, CDOF), 1)
    trace = [jnp.zeros((CDOF, CDOF), F32), jnp.zeros((CDOF, CDOF), F32)]
    square = jnp.zeros((CDOF, CDOF), F32)
    for slab in range(nt):
        for part in range(2):
            block = col_v[slab, part].astype(F32)
            trace[part] = trace[part] + block
            square = square + block * block
    scale = 1.0 / (nt * nz * nx * CDOF)
    stats = [jnp.where(eye, trace[0], 0.0), jnp.where(eye, trace[1], 0.0), square]
    stats = [jnp.sum(row_sum(value), axis=1, keepdims=True) * scale for value in stats]
    stats = jnp.concatenate([jnp.broadcast_to(value, (1, LANES)) for value in stats], axis=0)

    for i in (1, 2):
        op_loads[i].wait()
        links_v[i] = pack_links(op_v.at[i])

    powers = [start]
    wide = apply_links(0)
    send_halo(1, wide)
    powers.append(first_group(wide))
    answers = nt - 1 - my_t + nz * nx - 1 - my_zx

    @pl.when(answers > 0)
    def _():
        pl.semaphore_wait(peers_in, answers)

    send_to_all(me_zx, zx_peers, stats, theta_buf, sum_send.at[0], sum_recv.at[0])
    wide = apply_links(1)
    ball_v[0] = split(wide)
    for i in reversed(range(1, len(sites))):
        pltpu.make_async_remote_copy(
            src_ref=ball_v.at[0],
            dst_ref=ball_v.at[i],
            send_sem=ball_send,
            recv_sem=ball_recv,
            device_id=ball_peers[i],
            device_id_type=MESH,
        ).start()
    powers.append(first_group(wide))

    sums_of(0, theta_buf, nz * nx, zx_peers[0]).wait_recv()
    stats = jnp.sum(theta_buf[...], axis=0)
    square = stats[2:3]
    inverse = jnp.where(square > 0.0, lax.rsqrt(jnp.where(square > 0.0, square, 1.0)), 1.0)
    theta = (stats[0:1] * inverse, stats[1:2] * inverse)
    weights = [inverse]
    for _ in range(3):
        weights.append(weights[-1] * inverse)

    def times_theta(field):
        return theta[0] * field + theta[1] * times_i(field)

    v1, v2 = powers[1] * weights[0], powers[2] * weights[1]
    one = [v1 - times_theta(start), v2 - times_theta(v1)]
    two = one[1] - times_theta(one[0])
    basis = [start, one[0], two]
    images = [v1, two + times_theta(one[0])]
    turned = [times_i(image) for image in images]
    start_turned = times_i(start)
    last_one, last_two, last_three = times_theta(v2), times_theta(one[1]), times_theta(two)

    def row_of(rows, first):
        table = jnp.concatenate(rows, axis=0)
        table = table + pltpu.roll(table, 64, 1)
        table = jnp.where(lane_iota(table.shape) < NRHS, table, 0.0)
        return row_sum(pltpu.roll(table, first * NRHS, 1, stride=NRHS, stride_axis=0))

    early = [row_sum(images[k] * images[k]) for k in range(2)]
    early += [row_sum(images[k] * start) for k in range(2)]
    early += [row_sum(turned[k] * start) for k in range(2)]
    early += [row_sum(images[0] * images[1]), row_sum(turned[0] * images[1])]
    early = row_of(early, 0)

    transfers(links_v.at[pl.ds(3, 4)], ball_peers[1], links_send, links_recv).wait_recv()
    transfers(ball_v.at[pl.ds(1, len(sites) - 1)], ball_peers[1], ball_send, ball_recv).wait_recv()

    def block(site, step=(0, 0, 0)):
        return ball_v[sites.index(shifted(site, step, sizes))]

    parts = []
    for i in range(7):
        own = block(sites[i])
        near = jnp.concatenate([own] * 3 + [block(sites[i], step) for step in steps[:2]], axis=0)
        far = jnp.concatenate([block(sites[i], step) for step in steps[2:]], axis=0)
        wide = times_links(links_v[i], near, far)
        parts.append(split(wide))
        if i == 0:
            v3 = first_group(wide) * weights[2]
    near = jnp.concatenate([parts[0]] * 3 + parts[1:3], axis=0)
    v4 = first_group(times_links(links_v[0], near, jnp.concatenate(parts[3:], axis=0))) * weights[3]

    one.append(v3 - last_one)
    two_next = one[2] - last_two
    basis.append(two_next - last_three)
    images.append(basis[3] + last_three)
    turned.append(times_i(images[2]))
    images.append(v4 - times_theta(v3) - times_theta(one[2]) - times_theta(two_next))
    late = [row_sum(images[k] * images[k]) for k in (2, 3)]
    late += [row_sum(images[k] * start) for k in (2, 3)]
    late += [row_sum(turned[2] * start), -row_sum(images[3] * start_turned)]
    late += [row_sum(images[i] * images[2]) for i in (0, 1)]
    late += [row_sum(images[i] * images[3]) for i in (0, 1, 2)]
    late += [row_sum(turned[i] * images[2]) for i in (0, 1)]
    late += [row_sum(turned[i] * images[3]) for i in (0, 1, 2)]
    dense = jnp.concatenate([early, row_of(late[:8], 0), row_of(late[8:], 0)], axis=0)

    send_to_all(t, t_peers, dense, t_buf, sum_send.at[1], sum_recv.at[1])
    turned.append(times_i(images[3]))
    basis_turned = [times_i(field) for field in basis]
    sums_of(1, t_buf, nt, t_peers[0]).wait_recv()
    dense = jnp.sum(t_buf[...], axis=0)
    send_to_all(me_zx, zx_peers, dense, zx_buf, sum_send.at[2], sum_recv.at[2])
    sums_of(2, zx_buf, nz * nx, zx_peers[0]).wait_recv()
    dense = jnp.sum(zx_buf[...], axis=0)

    sums = []
    for g in range(3):
        spread = pltpu.roll(jnp.broadcast_to(dense[g : g + 1], (8, LANES)), 0, 1, stride=NRHS, stride_axis=0)
        sums += [spread[(8 - i) % 8 : (8 - i) % 8 + 1] for i in range(8)]
    diag = sums[0:2] + sums[8:10]
    right = [(sums[2], sums[4]), (sums[3], sums[5]), (sums[10], sums[12]), (sums[11], sums[13])]
    upper = {
        (0, 1): (sums[6], sums[7]),
        (0, 2): (sums[14], sums[19]),
        (1, 2): (sums[15], sums[20]),
        (0, 3): (sums[16], sums[21]),
        (1, 3): (sums[17], sums[22]),
        (2, 3): (sums[18], sums[23]),
    }
    coef = [(both_halves(c[0]), both_halves(c[1])) for c in solve(diag, upper, right)]

    field = None
    remain = start
    for k in range(4):
        cr, ci = coef[k]
        term = (cr * basis[k] + ci * basis_turned[k]) * inverse
        field = term if field is None else field + term
        remain = remain - cr * images[k] - ci * turned[k]
    x_ref[...] = field
    r_ref[...] = remain

    transfers(links_v.at[pl.ds(3, 4)], ball_peers[1], links_send, links_recv).wait_send()
    transfers(ball_v.at[pl.ds(1, len(sites) - 1)], ball_peers[1], ball_send, ball_recv).wait_send()
    for k in range(2):
        transfers(cells.at[k, pl.ds(3, 6)], slots[0][1], halo_send.at[k], halo_recv.at[k]).wait_send()
    sums_of(0, theta_buf, nz * nx, zx_peers[0]).wait_send()
    sums_of(1, t_buf, nt, t_peers[0]).wait_send()
    sums_of(2, zx_buf, nz * nx, zx_peers[0]).wait_send()


def prolong_kernel(x_ref, r_ref, basis_ref, out_ref, remain_ref, rows_v):
    x = x_ref[...].astype(BF16).astype(F32)
    upper, lower = x[:NVEC], x[NVEC:]
    every = upper + pltpu.roll(upper, NRHS, 1) + pltpu.roll(lower, 2 * NRHS, 1) + pltpu.roll(lower, 3 * NRHS, 1)
    every = jnp.concatenate([every, times_i(every)], axis=0)
    group = group_of(every.shape)
    for s in range(4):
        rows_v[pl.ds(s, 2 * NVEC, stride=4), :] = jnp.where(group == s, every, 0.0)
    weights = rows_v[...].T.astype(BF16)
    for colour in range(3):
        value = jnp.dot(weights, basis_ref[colour], preferred_element_type=F32)
        out_ref[:, :, colour] = value.astype(BF16).reshape(2, 4, NRHS, 512)
    turned = r_ref[...].T
    remain_ref[0] = turned[0:NRHS]
    remain_ref[1] = turned[64 : 64 + NRHS]


def body(sizes, residual, null_vectors, coarse_op):
    sites = residual.shape[-1]
    res = residual.reshape(2, 4, 3, NRHS, sites)
    nv = null_vectors.transpose(0, 1, 3, 4, 5, 6, 2, 7).reshape(2, NVEC, 3, 4, sites)
    nt, nz, nx = sizes
    any_spec = pl.BlockSpec(memory_space=pltpu.HBM)
    vmem_spec = pl.BlockSpec(memory_space=pltpu.VMEM)
    field = jax.ShapeDtypeStruct((CDOF, LANES), F32)
    far = [pltpu.with_memory_space_constraint(a, pltpu.HBM) for a in (res, nv, coarse_op)]
    x, r, basis = pl.pallas_call(
        functools.partial(coarse_kernel, sizes),
        out_shape=(field, field, jax.ShapeDtypeStruct((3, 2 * NVEC * 4, sites), BF16)),
        in_specs=[any_spec] * 3,
        out_specs=(vmem_spec,) * 3,
        scratch_shapes=[
            pltpu.VMEM((3, 2, 4, NRHS, sites), BF16),
            pltpu.VMEM((3, 2, NVEC, 4, sites), BF16),
            pltpu.VMEM((3, LINKS, 2, CDOF, CDOF), BF16),
            pltpu.VMEM((nt, 2, CDOF, CDOF), BF16),
            pltpu.VMEM((2 * NVEC * 4, LANES), F32),
            pltpu.VMEM((2, LINKS, CDOF, LANES), BF16),
            pltpu.VMEM((7, 2 * CDOF, 512), BF16),
            pltpu.VMEM((len(ball(sizes)[1]), CDOF, LANES), BF16),
            pltpu.VMEM((nz * nx, 3, LANES), F32),
            pltpu.VMEM((nt, 3, LANES), F32),
            pltpu.VMEM((nz * nx, 3, LANES), F32),
            pltpu.SemaphoreType.DMA((10,)),
            pltpu.SemaphoreType.DMA((2,)),
            pltpu.SemaphoreType.DMA((2,)),
            pltpu.SemaphoreType.DMA((2,)),
            pltpu.SemaphoreType.DMA((3,)),
            pltpu.SemaphoreType.DMA((3,)),
            pltpu.SemaphoreType.REGULAR,
            pltpu.SemaphoreType.DMA,
            pltpu.SemaphoreType.DMA,
            pltpu.SemaphoreType.DMA,
            pltpu.SemaphoreType.DMA,
        ],
        compiler_params=pltpu.CompilerParams(
            collective_id=0, has_side_effects=True, vmem_limit_bytes=16 * 1024 * 1024
        ),
    )(*far)
    correction, remain = pl.pallas_call(
        prolong_kernel,
        out_shape=(
            jax.ShapeDtypeStruct((2, 4, 3, NRHS, sites), BF16),
            jax.ShapeDtypeStruct((2, NRHS, CDOF), F32),
        ),
        in_specs=[vmem_spec] * 3,
        out_specs=(vmem_spec, vmem_spec),
        scratch_shapes=[pltpu.VMEM((2 * NVEC * 4, LANES), F32)],
        compiler_params=pltpu.CompilerParams(vmem_limit_bytes=16 * 1024 * 1024),
    )(x, r, basis)
    correction = correction.reshape(2, 4, 3, NRHS, 1, 1, 1, sites)
    remain = remain.transpose(0, 2, 1).reshape(2, CDOF, 1, 1, 1, NRHS)
    return correction, remain


def solution(mesh):
    sizes = (mesh.shape["ta"], mesh.shape["gz"], mesh.shape["gy"])
    return jax.shard_map(
        functools.partial(body, sizes),
        mesh=mesh,
        in_specs=(
            P(None, None, None, None, "ta", "gz", "gy", None),
            P(None, None, None, None, "ta", "gz", "gy", None),
            P(None, "gz", "gy", None, None, None, None),
        ),
        out_specs=(
            P(None, None, None, None, "ta", "gz", "gy", None),
            P(None, None, "ta", "gz", "gy", None),
        ),
        check_vma=False,
    )
```

```python
import functools

import jax
import jax.numpy as jnp
from jax import lax
from jax.experimental import pallas as pl
from jax.experimental.pallas import tpu as pltpu
from jax.sharding import PartitionSpec as P

MESH = pl.DeviceIdType.MESH
F32 = jnp.float32
BF16 = jnp.bfloat16
CDOF = 48
NVEC = 24
NRHS = 16
LINKS = 9
LANES = 128


def lane_iota(shape):
    return lax.broadcasted_iota(jnp.int32, shape, len(shape) - 1)


def group_of(shape):
    return lax.rem(lax.div(lane_iota(shape), NRHS), 4)


def sign_of(shape):
    return jnp.where(lane_iota(shape) < 64, -1.0, 1.0).astype(F32)


def times_i(field):
    return sign_of(field.shape) * pltpu.roll(field, 64, 1)


def restrict(loads, nv_ref, res_ref, basis_ref, rows_ref):
    total = None
    for colour in range(3):
        for load in loads[colour]:
            load.wait()
        basis = nv_ref[colour].reshape(2 * NVEC * 4, 512)
        basis_ref[colour] = basis
        source = res_ref[colour].reshape(2 * 4 * NRHS, 512)
        part = lax.dot_general(basis, source, (((1,), (1,)), ((), ())), preferred_element_type=F32)
        total = part if total is None else total + part
    rows_ref[...] = total
    by_spin = [rows_ref[pl.ds(s, 2 * NVEC, stride=4), :] for s in range(4)]
    group = group_of((2 * NVEC, LANES))
    halves = []
    for chirality in range(2):
        a, b = 2 * chirality, 2 * chirality + 1
        picked = jnp.where(group == a, by_spin[a], jnp.where(group == b, by_spin[b], 0.0))
        picked = picked + pltpu.roll(picked, LANES - NRHS, 1)
        if chirality == 1:
            picked = pltpu.roll(picked, LANES - 2 * NRHS, 1)
        halves.append(picked[:NVEC] - times_i(picked[NVEC:]))
    field = jnp.concatenate(halves, axis=0)
    return jnp.where(group == 0, field, 0.0)


def split(wide):
    group = group_of(wide.shape)
    high = wide.astype(BF16).astype(F32)
    return jnp.where(group == 0, high, jnp.where(group == 2, wide - high, 0.0)).astype(BF16)


def both_groups(field):
    return field + pltpu.roll(field, 2 * NRHS, 1)


def combine(product):
    real, imag = product[:CDOF], product[CDOF:]
    first = group_of(real.shape) == 0
    back, forth = LANES - 2 * NRHS, 2 * NRHS
    total = real + jnp.where(first, pltpu.roll(real, back, 1), pltpu.roll(real, forth, 1))
    cross = pltpu.roll(imag, 64, 1) + jnp.where(first, pltpu.roll(imag, forth, 1), pltpu.roll(imag, back, 1))
    return total + sign_of(real.shape) * cross


def first_group(wide):
    return jnp.where(group_of(wide.shape) == 0, wide, 0.0)


def row_sum(product):
    return jnp.sum(product, axis=0, keepdims=True)


def cmul(a, b):
    return a[0] * b[0] - a[1] * b[1], a[0] * b[1] + a[1] * b[0]


def cmul_conj(a, b):
    return a[0] * b[0] + a[1] * b[1], a[0] * b[1] - a[1] * b[0]


def csub(a, b):
    return a[0] - b[0], a[1] - b[1]


def solve(diag, upper, right):
    n = len(diag)
    d, inv, low = [], [], {}
    for j in range(n):
        value = diag[j]
        for k in range(j):
            value = value - d[k] * (low[j, k][0] ** 2 + low[j, k][1] ** 2)
        d.append(value)
        inv.append(1.0 / value)
        for i in range(j + 1, n):
            entry = (upper[j, i][0], -upper[j, i][1])
            for k in range(j):
                term = cmul_conj(low[j, k], low[i, k])
                entry = csub(entry, (d[k] * term[0], d[k] * term[1]))
            low[i, j] = (entry[0] * inv[j], entry[1] * inv[j])
    y = []
    for i in range(n):
        value = right[i]
        for k in range(i):
            value = csub(value, cmul(low[i, k], y[k]))
        y.append(value)
    c = [None] * n
    for i in reversed(range(n)):
        value = (y[i][0] * inv[i], y[i][1] * inv[i])
        for k in range(i + 1, n):
            value = csub(value, cmul_conj(low[k, i], c[k]))
        c[i] = value
    return c


def both_halves(row):
    row = jnp.where(lane_iota(row.shape) < NRHS, row, 0.0)
    return row + pltpu.roll(row, 64, 1)


def others(count, me):
    return [k + jnp.where(k >= me, 1, 0) for k in range(count - 1)]


def rank_of(t, nt):
    half = nt // 2
    y = lax.div(t, 2)
    r = jnp.where(y == 0, 0, jnp.where(y <= half // 2, 2 * y - 1, 2 * (half - y)))
    return 2 * r + lax.rem(t, 2)


def slab_of(rank, nt):
    half = nt // 2
    r = lax.div(rank, 2)
    y = jnp.where(lax.rem(r, 2) == 1, lax.div(r + 1, 2), lax.rem(half - lax.div(r, 2), half))
    return 2 * y + lax.rem(rank, 2)


def ball(sizes):
    steps = [(1, 0, 0), (-1, 0, 0), (0, 1, 0), (0, -1, 0), (0, 0, 1), (0, 0, -1)]
    found = [(0, 0, 0)] + [shifted((0, 0, 0), step, sizes) for step in steps]
    for a in steps:
        for b in steps:
            site = shifted(shifted((0, 0, 0), a, sizes), b, sizes)
            if site not in found:
                found.append(site)
    return steps, found


def shifted(site, step, sizes):
    return tuple((a + b) % n for a, b, n in zip(site, step, sizes))


def pack_links(op_ref):
    def rows(part):
        blocks = [op_ref[m, part].astype(F32) for m in range(LINKS)]
        own = blocks[0] + (blocks[7] + blocks[8])
        high = own.astype(BF16).astype(F32)
        return jnp.concatenate([high, own - high] + blocks[1:7], axis=1)

    return jnp.concatenate([rows(0), rows(1)], axis=0).astype(BF16)


def times_links(links, blocks):
    field = jnp.concatenate([blocks[0]] + blocks, axis=0)
    return combine(jnp.dot(links[...], field, preferred_element_type=F32))


def send_to_all(me, peers, value, buf, send_sem, recv_sem):
    buf[me] = value
    for peer in peers:
        pltpu.make_async_remote_copy(
            src_ref=buf.at[me],
            dst_ref=buf.at[me],
            send_sem=send_sem,
            recv_sem=recv_sem,
            device_id=peer,
            device_id_type=MESH,
        ).start()


def transfers(block, peer, send_sem, recv_sem):
    return pltpu.make_async_remote_copy(
        src_ref=block, dst_ref=block, send_sem=send_sem, recv_sem=recv_sem, device_id=peer, device_id_type=MESH
    )


def coarse_kernel(
    sizes,
    res_hbm,
    nv_hbm,
    op_hbm,
    x_ref,
    r_ref,
    basis_ref,
    res_v,
    nv_v,
    op_v,
    col_v,
    rows_v,
    links_v,
    ball_v,
    theta_buf,
    t_buf,
    zx_buf,
    local_sem,
    sum_send,
    sum_recv,
    peers_in,
    links_send,
    links_recv,
    ball_send,
    ball_recv,
):
    nt, nz, nx = sizes
    t, z, x = lax.axis_index("ta"), lax.axis_index("gz"), lax.axis_index("gy")
    me_zx = z * nx + x
    loads = [
        (
            pltpu.make_async_copy(nv_hbm.at[:, :, colour], nv_v.at[colour], local_sem.at[2 * colour]),
            pltpu.make_async_copy(res_hbm.at[:, :, colour], res_v.at[colour], local_sem.at[2 * colour + 1]),
        )
        for colour in range(3)
    ]
    op_loads = [
        pltpu.make_async_copy(op_hbm.at[slab, 0, 0], op_v.at[i], local_sem.at[6 + i])
        for i, slab in enumerate((t, lax.rem(t + 1, nt), lax.rem(t + nt - 1, nt)))
    ]
    col_load = pltpu.make_async_copy(op_hbm.at[:, 0, 0, 0], col_v, local_sem.at[9])
    steps, sites = ball(sizes)
    ball_peers = [
        (lax.rem(t + nt - a, nt), lax.rem(z + nz - b, nz), lax.rem(x + nx - c, nx)) for a, b, c in sites
    ]
    my_t, my_zx = rank_of(t, nt), me_zx

    def t_peer(rank):
        return slab_of(rank, nt), z, x

    def zx_peer(rank):
        return t, lax.div(rank, nx), lax.rem(rank, nx)

    def signal_peers(semaphore, t_ranks, zx_ranks):
        for ranks, peer in ((t_ranks, t_peer), (zx_ranks, zx_peer)):
            def step(rank, carry, peer=peer):
                pl.semaphore_signal(semaphore, inc=1, device_id=peer(rank), device_id_type=MESH)
                return carry
            lax.fori_loop(*ranks, step, 0)

    barrier = pltpu.get_barrier_semaphore()
    op_loads[0].start()
    for pair in loads:
        for load in pair:
            load.start()
    for peer in ball_peers[1:]:
        pl.semaphore_signal(barrier, inc=1, device_id=peer, device_id_type=MESH)
    signal_peers(barrier, (my_t + 1, nt), (my_zx + 1, nz * nx))
    t_peers = [t_peer(k) for k in others(nt, my_t)]
    zx_peers = [zx_peer(k) for k in others(nz * nx, my_zx)]

    for load in op_loads[1:]:
        load.start()
    col_load.start()

    start = restrict(loads, nv_v, res_v, basis_ref, rows_v)

    def send_ball(k, wide):
        ball_v[k, 0] = split(wide)
        for i in reversed(range(1, len(sites))):
            pltpu.make_async_remote_copy(
                src_ref=ball_v.at[k, 0],
                dst_ref=ball_v.at[k, i],
                send_sem=ball_send.at[k],
                recv_sem=ball_recv.at[k],
                device_id=ball_peers[i],
                device_id_type=MESH,
            ).start()

    def ball_transfers(k):
        block = ball_v.at[k, pl.ds(1, len(sites) - 1)]
        return transfers(block, ball_peers[1], ball_send.at[k], ball_recv.at[k])

    def apply_twice(k):
        ball_transfers(k).wait_recv()

        def block(site, step=(0, 0, 0)):
            return ball_v[k, sites.index(shifted(site, step, sizes))]

        parts = []
        for i in range(7):
            wide = times_links(links_v.at[i], [block(sites[i], step) for step in [(0, 0, 0)] + steps])
            parts.append(split(wide))
            if i == 0:
                once = wide
        return once, times_links(links_v.at[0], parts)

    def sums_of(k, buf, count, peer):
        return transfers(buf.at[pl.ds(0, count - 1)], peer, sum_send.at[k], sum_recv.at[k])

    pl.semaphore_wait(barrier, len(sites) - 1 + my_t + my_zx)
    send_ball(0, both_groups(start))
    op_loads[0].wait()
    links_v[0] = pack_links(op_v.at[0])
    for i in range(3, 7):
        pltpu.make_async_remote_copy(
            src_ref=links_v.at[0],
            dst_ref=links_v.at[i],
            send_sem=links_send,
            recv_sem=links_recv,
            device_id=ball_peers[i],
            device_id_type=MESH,
        ).start()
    signal_peers(peers_in, (0, my_t), (0, my_zx))

    col_load.wait()
    eye = lax.broadcasted_iota(jnp.int32, (CDOF, CDOF), 0) == lax.broadcasted_iota(jnp.int32, (CDOF, CDOF), 1)
    trace = [jnp.zeros((CDOF, CDOF), F32), jnp.zeros((CDOF, CDOF), F32)]
    square = jnp.zeros((CDOF, CDOF), F32)
    for slab in range(nt):
        for part in range(2):
            block = col_v[slab, part].astype(F32)
            trace[part] = trace[part] + block
            square = square + block * block
    scale = 1.0 / (nt * nz * nx * CDOF)
    stats = [jnp.where(eye, trace[0], 0.0), jnp.where(eye, trace[1], 0.0), square]
    stats = [jnp.sum(row_sum(value), axis=1, keepdims=True) * scale for value in stats]
    stats = jnp.concatenate([jnp.broadcast_to(value, (1, LANES)) for value in stats], axis=0)

    for i in (1, 2):
        op_loads[i].wait()
        links_v[i] = pack_links(op_v.at[i])

    answers = nt - 1 - my_t + nz * nx - 1 - my_zx

    @pl.when(answers > 0)
    def _():
        pl.semaphore_wait(peers_in, answers)

    send_to_all(me_zx, zx_peers, stats, theta_buf, sum_send.at[0], sum_recv.at[0])
    transfers(links_v.at[pl.ds(3, 4)], ball_peers[1], links_send, links_recv).wait_recv()
    once, twice = apply_twice(0)
    send_ball(1, twice)
    powers = [start, first_group(once), first_group(twice)]

    sums_of(0, theta_buf, nz * nx, zx_peers[0]).wait_recv()
    stats = jnp.sum(theta_buf[...], axis=0)
    square = stats[2:3]
    inverse = jnp.where(square > 0.0, lax.rsqrt(jnp.where(square > 0.0, square, 1.0)), 1.0)
    theta = (stats[0:1] * inverse, stats[1:2] * inverse)
    weights = [inverse]
    for _ in range(3):
        weights.append(weights[-1] * inverse)

    def times_theta(field):
        return theta[0] * field + theta[1] * times_i(field)

    v1, v2 = powers[1] * weights[0], powers[2] * weights[1]
    one = [v1 - times_theta(start), v2 - times_theta(v1)]
    two = one[1] - times_theta(one[0])
    basis = [start, one[0], two]
    images = [v1, two + times_theta(one[0])]
    turned = [times_i(image) for image in images]
    start_turned = times_i(start)
    last_one, last_two, last_three = times_theta(v2), times_theta(one[1]), times_theta(two)

    def row_of(rows, first):
        table = jnp.concatenate(rows, axis=0)
        table = table + pltpu.roll(table, 64, 1)
        table = jnp.where(lane_iota(table.shape) < NRHS, table, 0.0)
        return row_sum(pltpu.roll(table, first * NRHS, 1, stride=NRHS, stride_axis=0))

    early = [row_sum(images[k] * images[k]) for k in range(2)]
    early += [row_sum(images[k] * start) for k in range(2)]
    early += [row_sum(turned[k] * start) for k in range(2)]
    early += [row_sum(images[0] * images[1]), row_sum(turned[0] * images[1])]
    early = row_of(early, 0)

    once, twice = apply_twice(1)
    v3, v4 = first_group(once) * weights[2], first_group(twice) * weights[3]

    one.append(v3 - last_one)
    two_next = one[2] - last_two
    basis.append(two_next - last_three)
    images.append(basis[3] + last_three)
    turned.append(times_i(images[2]))
    images.append(v4 - times_theta(v3) - times_theta(one[2]) - times_theta(two_next))
    late = [row_sum(images[k] * images[k]) for k in (2, 3)]
    late += [row_sum(images[k] * start) for k in (2, 3)]
    late += [row_sum(turned[2] * start), -row_sum(images[3] * start_turned)]
    late += [row_sum(images[i] * images[2]) for i in (0, 1)]
    late += [row_sum(images[i] * images[3]) for i in (0, 1, 2)]
    late += [row_sum(turned[i] * images[2]) for i in (0, 1)]
    late += [row_sum(turned[i] * images[3]) for i in (0, 1, 2)]
    dense = jnp.concatenate([early, row_of(late[:8], 0), row_of(late[8:], 0)], axis=0)

    send_to_all(t, t_peers, dense, t_buf, sum_send.at[1], sum_recv.at[1])
    turned.append(times_i(images[3]))
    basis_turned = [times_i(field) for field in basis]
    sums_of(1, t_buf, nt, t_peers[0]).wait_recv()
    dense = jnp.sum(t_buf[...], axis=0)
    send_to_all(me_zx, zx_peers, dense, zx_buf, sum_send.at[2], sum_recv.at[2])
    sums_of(2, zx_buf, nz * nx, zx_peers[0]).wait_recv()
    dense = jnp.sum(zx_buf[...], axis=0)

    sums = []
    for g in range(3):
        spread = pltpu.roll(jnp.broadcast_to(dense[g : g + 1], (8, LANES)), 0, 1, stride=NRHS, stride_axis=0)
        sums += [spread[(8 - i) % 8 : (8 - i) % 8 + 1] for i in range(8)]
    diag = sums[0:2] + sums[8:10]
    right = [(sums[2], sums[4]), (sums[3], sums[5]), (sums[10], sums[12]), (sums[11], sums[13])]
    upper = {
        (0, 1): (sums[6], sums[7]),
        (0, 2): (sums[14], sums[19]),
        (1, 2): (sums[15], sums[20]),
        (0, 3): (sums[16], sums[21]),
        (1, 3): (sums[17], sums[22]),
        (2, 3): (sums[18], sums[23]),
    }
    coef = [(both_halves(c[0]), both_halves(c[1])) for c in solve(diag, upper, right)]

    field = None
    remain = start
    for k in range(4):
        cr, ci = coef[k]
        term = (cr * basis[k] + ci * basis_turned[k]) * inverse
        field = term if field is None else field + term
        remain = remain - cr * images[k] - ci * turned[k]
    x_ref[...] = field
    r_ref[...] = remain

    transfers(links_v.at[pl.ds(3, 4)], ball_peers[1], links_send, links_recv).wait_send()
    ball_transfers(0).wait_send()
    ball_transfers(1).wait_send()
    sums_of(0, theta_buf, nz * nx, zx_peers[0]).wait_send()
    sums_of(1, t_buf, nt, t_peers[0]).wait_send()
    sums_of(2, zx_buf, nz * nx, zx_peers[0]).wait_send()


def prolong_kernel(x_ref, r_ref, basis_ref, out_ref, remain_ref, rows_v):
    x = x_ref[...].astype(BF16).astype(F32)
    upper, lower = x[:NVEC], x[NVEC:]
    every = upper + pltpu.roll(upper, NRHS, 1) + pltpu.roll(lower, 2 * NRHS, 1) + pltpu.roll(lower, 3 * NRHS, 1)
    every = jnp.concatenate([every, times_i(every)], axis=0)
    group = group_of(every.shape)
    for s in range(4):
        rows_v[pl.ds(s, 2 * NVEC, stride=4), :] = jnp.where(group == s, every, 0.0)
    weights = rows_v[...].T.astype(BF16)
    for colour in range(3):
        value = jnp.dot(weights, basis_ref[colour], preferred_element_type=F32)
        out_ref[:, :, colour] = value.astype(BF16).reshape(2, 4, NRHS, 512)
    turned = r_ref[...].T
    remain_ref[0] = turned[0:NRHS]
    remain_ref[1] = turned[64 : 64 + NRHS]


def body(sizes, residual, null_vectors, coarse_op):
    sites = residual.shape[-1]
    res = residual.reshape(2, 4, 3, NRHS, sites)
    nv = null_vectors.transpose(0, 1, 3, 4, 5, 6, 2, 7).reshape(2, NVEC, 3, 4, sites)
    nt, nz, nx = sizes
    any_spec = pl.BlockSpec(memory_space=pltpu.HBM)
    vmem_spec = pl.BlockSpec(memory_space=pltpu.VMEM)
    field = jax.ShapeDtypeStruct((CDOF, LANES), F32)
    far = [pltpu.with_memory_space_constraint(a, pltpu.HBM) for a in (res, nv, coarse_op)]
    x, r, basis = pl.pallas_call(
        functools.partial(coarse_kernel, sizes),
        out_shape=(field, field, jax.ShapeDtypeStruct((3, 2 * NVEC * 4, sites), BF16)),
        in_specs=[any_spec] * 3,
        out_specs=(vmem_spec,) * 3,
        scratch_shapes=[
            pltpu.VMEM((3, 2, 4, NRHS, sites), BF16),
            pltpu.VMEM((3, 2, NVEC, 4, sites), BF16),
            pltpu.VMEM((3, LINKS, 2, CDOF, CDOF), BF16),
            pltpu.VMEM((nt, 2, CDOF, CDOF), BF16),
            pltpu.VMEM((2 * NVEC * 4, LANES), F32),
            pltpu.VMEM((7, 2 * CDOF, 8 * CDOF), BF16),
            pltpu.VMEM((2, len(ball(sizes)[1]), CDOF, LANES), BF16),
            pltpu.VMEM((nz * nx, 3, LANES), F32),
            pltpu.VMEM((nt, 3, LANES), F32),
            pltpu.VMEM((nz * nx, 3, LANES), F32),
            pltpu.SemaphoreType.DMA((10,)),
            pltpu.SemaphoreType.DMA((3,)),
            pltpu.SemaphoreType.DMA((3,)),
            pltpu.SemaphoreType.REGULAR,
            pltpu.SemaphoreType.DMA,
            pltpu.SemaphoreType.DMA,
            pltpu.SemaphoreType.DMA((2,)),
            pltpu.SemaphoreType.DMA((2,)),
        ],
        compiler_params=pltpu.CompilerParams(
            collective_id=0, has_side_effects=True, vmem_limit_bytes=16 * 1024 * 1024
        ),
    )(*far)
    correction, remain = pl.pallas_call(
        prolong_kernel,
        out_shape=(
            jax.ShapeDtypeStruct((2, 4, 3, NRHS, sites), BF16),
            jax.ShapeDtypeStruct((2, NRHS, CDOF), F32),
        ),
        in_specs=[vmem_spec] * 3,
        out_specs=(vmem_spec, vmem_spec),
        scratch_shapes=[pltpu.VMEM((2 * NVEC * 4, LANES), F32)],
        compiler_params=pltpu.CompilerParams(vmem_limit_bytes=16 * 1024 * 1024),
    )(x, r, basis)
    correction = correction.reshape(2, 4, 3, NRHS, 1, 1, 1, sites)
    remain = remain.transpose(0, 2, 1).reshape(2, CDOF, 1, 1, 1, NRHS)
    return correction, remain


def solution(mesh):
    sizes = (mesh.shape["ta"], mesh.shape["gz"], mesh.shape["gy"])
    return jax.shard_map(
        functools.partial(body, sizes),
        mesh=mesh,
        in_specs=(
            P(None, None, None, None, "ta", "gz", "gy", None),
            P(None, None, None, None, "ta", "gz", "gy", None),
            P(None, "gz", "gy", None, None, None, None),
        ),
        out_specs=(
            P(None, None, None, None, "ta", "gz", "gy", None),
            P(None, None, "ta", "gz", "gy", None),
        ),
        check_vma=False,
    )
```

```python
import functools

import jax
import jax.numpy as jnp
from jax import lax
from jax.experimental import pallas as pl
from jax.experimental.pallas import tpu as pltpu
from jax.sharding import PartitionSpec as P

MESH = pl.DeviceIdType.MESH
F32 = jnp.float32
BF16 = jnp.bfloat16
CDOF = 48
NVEC = 24
NRHS = 16
LINKS = 9
LANES = 128


def lane_iota(shape):
    return lax.broadcasted_iota(jnp.int32, shape, len(shape) - 1)


def group_of(shape):
    return lax.rem(lax.div(lane_iota(shape), NRHS), 4)


def sign_of(shape):
    return jnp.where(lane_iota(shape) < 64, -1.0, 1.0).astype(F32)


def times_i(field):
    return sign_of(field.shape) * pltpu.roll(field, 64, 1)


def restrict(loads, nv_ref, res_ref, basis_ref, rows_ref):
    total = None
    for colour in range(3):
        for load in loads[colour]:
            load.wait()
        basis = nv_ref[colour].reshape(2 * NVEC * 4, 512)
        basis_ref[colour] = basis
        source = res_ref[colour].reshape(2 * 4 * NRHS, 512)
        part = lax.dot_general(basis, source, (((1,), (1,)), ((), ())), preferred_element_type=F32)
        total = part if total is None else total + part
    rows_ref[...] = total
    by_spin = [rows_ref[pl.ds(s, 2 * NVEC, stride=4), :] for s in range(4)]
    group = group_of((2 * NVEC, LANES))
    halves = []
    for chirality in range(2):
        a, b = 2 * chirality, 2 * chirality + 1
        picked = jnp.where(group == a, by_spin[a], jnp.where(group == b, by_spin[b], 0.0))
        picked = picked + pltpu.roll(picked, LANES - NRHS, 1)
        if chirality == 1:
            picked = pltpu.roll(picked, LANES - 2 * NRHS, 1)
        halves.append(picked[:NVEC] - times_i(picked[NVEC:]))
    field = jnp.concatenate(halves, axis=0)
    return jnp.where(group == 0, field, 0.0)


def split(wide):
    group = group_of(wide.shape)
    high = wide.astype(BF16).astype(F32)
    return jnp.where(group == 0, high, jnp.where(group == 2, wide - high, 0.0)).astype(BF16)


def both_groups(field):
    return field + pltpu.roll(field, 2 * NRHS, 1)


def combine(product):
    real, imag = product[:CDOF], product[CDOF:]
    first = group_of(real.shape) == 0
    back, forth = LANES - 2 * NRHS, 2 * NRHS
    total = real + jnp.where(first, pltpu.roll(real, back, 1), pltpu.roll(real, forth, 1))
    cross = pltpu.roll(imag, 64, 1) + jnp.where(first, pltpu.roll(imag, forth, 1), pltpu.roll(imag, back, 1))
    return total + sign_of(real.shape) * cross


def first_group(wide):
    return jnp.where(group_of(wide.shape) == 0, wide, 0.0)


def row_sum(product):
    return jnp.sum(product, axis=0, keepdims=True)


def cmul(a, b):
    return a[0] * b[0] - a[1] * b[1], a[0] * b[1] + a[1] * b[0]


def cmul_conj(a, b):
    return a[0] * b[0] + a[1] * b[1], a[0] * b[1] - a[1] * b[0]


def csub(a, b):
    return a[0] - b[0], a[1] - b[1]


def solve(diag, upper, right):
    n = len(diag)
    d, inv, low = [], [], {}
    for j in range(n):
        value = diag[j]
        for k in range(j):
            value = value - d[k] * (low[j, k][0] ** 2 + low[j, k][1] ** 2)
        d.append(value)
        inv.append(1.0 / value)
        for i in range(j + 1, n):
            entry = (upper[j, i][0], -upper[j, i][1])
            for k in range(j):
                term = cmul_conj(low[j, k], low[i, k])
                entry = csub(entry, (d[k] * term[0], d[k] * term[1]))
            low[i, j] = (entry[0] * inv[j], entry[1] * inv[j])
    y = []
    for i in range(n):
        value = right[i]
        for k in range(i):
            value = csub(value, cmul(low[i, k], y[k]))
        y.append(value)
    c = [None] * n
    for i in reversed(range(n)):
        value = (y[i][0] * inv[i], y[i][1] * inv[i])
        for k in range(i + 1, n):
            value = csub(value, cmul_conj(low[k, i], c[k]))
        c[i] = value
    return c


def both_halves(row):
    row = jnp.where(lane_iota(row.shape) < NRHS, row, 0.0)
    return row + pltpu.roll(row, 64, 1)


def others(count, me):
    return [k + jnp.where(k >= me, 1, 0) for k in range(count - 1)]


def rank_of(t, nt):
    half = nt // 2
    y = lax.div(t, 2)
    r = jnp.where(y == 0, 0, jnp.where(y <= half // 2, 2 * y - 1, 2 * (half - y)))
    return 2 * r + lax.rem(t, 2)


def slab_of(rank, nt):
    half = nt // 2
    r = lax.div(rank, 2)
    y = jnp.where(lax.rem(r, 2) == 1, lax.div(r + 1, 2), lax.rem(half - lax.div(r, 2), half))
    return 2 * y + lax.rem(rank, 2)


def ball(sizes):
    steps = [(1, 0, 0), (-1, 0, 0), (0, 1, 0), (0, -1, 0), (0, 0, 1), (0, 0, -1)]
    found = [(0, 0, 0)] + [shifted((0, 0, 0), step, sizes) for step in steps]
    for a in steps:
        for b in steps:
            site = shifted(shifted((0, 0, 0), a, sizes), b, sizes)
            if site not in found:
                found.append(site)
    return steps, found


def shifted(site, step, sizes):
    return tuple((a + b) % n for a, b, n in zip(site, step, sizes))


def pack_links(op_ref):
    def rows(part):
        blocks = [op_ref[m, part].astype(F32) for m in range(LINKS)]
        own = blocks[0] + (blocks[7] + blocks[8])
        high = own.astype(BF16).astype(F32)
        return jnp.concatenate([high, own - high] + blocks[1:7], axis=1)

    return jnp.concatenate([rows(0), rows(1)], axis=0).astype(BF16)


def times_links(links, blocks):
    field = jnp.concatenate([blocks[0]] + blocks, axis=0)
    return combine(jnp.dot(links[...], field, preferred_element_type=F32))


def send_to_all(me, peers, value, buf, send_sem, recv_sem):
    buf[me] = value
    for peer in peers:
        pltpu.make_async_remote_copy(
            src_ref=buf.at[me],
            dst_ref=buf.at[me],
            send_sem=send_sem,
            recv_sem=recv_sem,
            device_id=peer,
            device_id_type=MESH,
        ).start()


def transfers(block, peer, send_sem, recv_sem):
    return pltpu.make_async_remote_copy(
        src_ref=block, dst_ref=block, send_sem=send_sem, recv_sem=recv_sem, device_id=peer, device_id_type=MESH
    )


def coarse_kernel(
    sizes,
    res_hbm,
    nv_hbm,
    op_hbm,
    x_ref,
    r_ref,
    basis_ref,
    res_v,
    nv_v,
    op_v,
    col_v,
    rows_v,
    links_v,
    ball_v,
    theta_buf,
    t_buf,
    zx_buf,
    local_sem,
    sum_send,
    sum_recv,
    t_in,
    zx_in,
    links_send,
    links_recv,
    ball_send,
    ball_recv,
):
    nt, nz, nx = sizes
    t, z, x = lax.axis_index("ta"), lax.axis_index("gz"), lax.axis_index("gy")
    me_zx = z * nx + x
    loads = [
        (
            pltpu.make_async_copy(nv_hbm.at[:, :, colour], nv_v.at[colour], local_sem.at[2 * colour]),
            pltpu.make_async_copy(res_hbm.at[:, :, colour], res_v.at[colour], local_sem.at[2 * colour + 1]),
        )
        for colour in range(3)
    ]
    op_loads = [
        pltpu.make_async_copy(op_hbm.at[slab, 0, 0], op_v.at[i], local_sem.at[6 + i])
        for i, slab in enumerate((t, lax.rem(t + 1, nt), lax.rem(t + nt - 1, nt)))
    ]
    col_load = pltpu.make_async_copy(op_hbm.at[:, 0, 0, 0], col_v, local_sem.at[9])
    steps, sites = ball(sizes)
    ball_peers = [
        (lax.rem(t + nt - a, nt), lax.rem(z + nz - b, nz), lax.rem(x + nx - c, nx)) for a, b, c in sites
    ]
    my_t, my_zx = rank_of(t, nt), me_zx

    def t_peer(rank):
        return slab_of(rank, nt), z, x

    def zx_peer(rank):
        return t, lax.div(rank, nx), lax.rem(rank, nx)

    def signal_peers(semaphore, peer, first, count):
        def step(rank, carry):
            pl.semaphore_signal(semaphore, inc=1, device_id=peer(rank), device_id_type=MESH)
            return carry

        lax.fori_loop(first, count, step, 0)

    def wait_peers(semaphore, count):
        @pl.when(count > 0)
        def _():
            pl.semaphore_wait(semaphore, count)

    barrier = pltpu.get_barrier_semaphore()
    op_loads[0].start()
    for pair in loads:
        for load in pair:
            load.start()
    for peer in ball_peers[1:]:
        pl.semaphore_signal(barrier, inc=1, device_id=peer, device_id_type=MESH)
    signal_peers(barrier, zx_peer, my_zx + 1, nz * nx)
    signal_peers(barrier, t_peer, my_t + 1, nt)
    t_peers = [t_peer(k) for k in others(nt, my_t)]
    zx_peers = [zx_peer(k) for k in others(nz * nx, my_zx)]

    for load in op_loads[1:]:
        load.start()
    col_load.start()

    op_loads[0].wait()
    links_v[0] = pack_links(op_v.at[0])
    start = restrict(loads, nv_v, res_v, basis_ref, rows_v)

    def send_ball(k, wide):
        ball_v[k, 0] = split(wide)
        for i in reversed(range(1, len(sites))):
            pltpu.make_async_remote_copy(
                src_ref=ball_v.at[k, 0],
                dst_ref=ball_v.at[k, i],
                send_sem=ball_send.at[k],
                recv_sem=ball_recv.at[k],
                device_id=ball_peers[i],
                device_id_type=MESH,
            ).start()

    def ball_transfers(k):
        block = ball_v.at[k, pl.ds(1, len(sites) - 1)]
        return transfers(block, ball_peers[1], ball_send.at[k], ball_recv.at[k])

    def apply_twice(k):
        ball_transfers(k).wait_recv()

        def block(site, step=(0, 0, 0)):
            return ball_v[k, sites.index(shifted(site, step, sizes))]

        parts = []
        for i in range(7):
            wide = times_links(links_v.at[i], [block(sites[i], step) for step in [(0, 0, 0)] + steps])
            parts.append(split(wide))
            if i == 0:
                once = wide
        return once, times_links(links_v.at[0], parts)

    def sums_of(k, buf, count, peer):
        return transfers(buf.at[pl.ds(0, count - 1)], peer, sum_send.at[k], sum_recv.at[k])

    pl.semaphore_wait(barrier, len(sites) - 1 + my_t + my_zx)
    send_ball(0, both_groups(start))
    for i in range(3, 7):
        pltpu.make_async_remote_copy(
            src_ref=links_v.at[0],
            dst_ref=links_v.at[i],
            send_sem=links_send,
            recv_sem=links_recv,
            device_id=ball_peers[i],
            device_id_type=MESH,
        ).start()
    signal_peers(zx_in, zx_peer, 0, my_zx)

    col_load.wait()
    eye = lax.broadcasted_iota(jnp.int32, (CDOF, CDOF), 0) == lax.broadcasted_iota(jnp.int32, (CDOF, CDOF), 1)
    trace = [jnp.zeros((CDOF, CDOF), F32), jnp.zeros((CDOF, CDOF), F32)]
    square = jnp.zeros((CDOF, CDOF), F32)
    for slab in range(nt):
        for part in range(2):
            block = col_v[slab, part].astype(F32)
            trace[part] = trace[part] + block
            square = square + block * block
    scale = 1.0 / (nt * nz * nx * CDOF)
    stats = [jnp.where(eye, trace[0], 0.0), jnp.where(eye, trace[1], 0.0), square]
    stats = [jnp.sum(row_sum(value), axis=1, keepdims=True) * scale for value in stats]
    stats = jnp.concatenate([jnp.broadcast_to(value, (1, LANES)) for value in stats], axis=0)

    for i in (1, 2):
        op_loads[i].wait()
        links_v[i] = pack_links(op_v.at[i])

    wait_peers(zx_in, nz * nx - 1 - my_zx)
    send_to_all(me_zx, zx_peers, stats, theta_buf, sum_send.at[0], sum_recv.at[0])
    transfers(links_v.at[pl.ds(3, 4)], ball_peers[1], links_send, links_recv).wait_recv()
    once, twice = apply_twice(0)
    send_ball(1, twice)
    signal_peers(t_in, t_peer, 0, my_t)
    powers = [start, first_group(once), first_group(twice)]

    sums_of(0, theta_buf, nz * nx, zx_peers[0]).wait_recv()
    stats = jnp.sum(theta_buf[...], axis=0)
    square = stats[2:3]
    inverse = jnp.where(square > 0.0, lax.rsqrt(jnp.where(square > 0.0, square, 1.0)), 1.0)
    theta = (stats[0:1] * inverse, stats[1:2] * inverse)
    weights = [inverse]
    for _ in range(3):
        weights.append(weights[-1] * inverse)

    def times_theta(field):
        return theta[0] * field + theta[1] * times_i(field)

    v1, v2 = powers[1] * weights[0], powers[2] * weights[1]
    one = [v1 - times_theta(start), v2 - times_theta(v1)]
    two = one[1] - times_theta(one[0])
    basis = [start, one[0], two]
    images = [v1, two + times_theta(one[0])]
    turned = [times_i(image) for image in images]
    start_turned = times_i(start)
    last_one, last_two, last_three = times_theta(v2), times_theta(one[1]), times_theta(two)

    def row_of(rows, first):
        table = jnp.concatenate(rows, axis=0)
        table = table + pltpu.roll(table, 64, 1)
        table = jnp.where(lane_iota(table.shape) < NRHS, table, 0.0)
        return row_sum(pltpu.roll(table, first * NRHS, 1, stride=NRHS, stride_axis=0))

    early = [row_sum(images[k] * images[k]) for k in range(2)]
    early += [row_sum(images[k] * start) for k in range(2)]
    early += [row_sum(turned[k] * start) for k in range(2)]
    early += [row_sum(images[0] * images[1]), row_sum(turned[0] * images[1])]
    early = row_of(early, 0)

    once, twice = apply_twice(1)
    v3, v4 = first_group(once) * weights[2], first_group(twice) * weights[3]

    one.append(v3 - last_one)
    two_next = one[2] - last_two
    basis.append(two_next - last_three)
    images.append(basis[3] + last_three)
    turned.append(times_i(images[2]))
    images.append(v4 - times_theta(v3) - times_theta(one[2]) - times_theta(two_next))
    late = [row_sum(images[k] * images[k]) for k in (2, 3)]
    late += [row_sum(images[k] * start) for k in (2, 3)]
    late += [row_sum(turned[2] * start), -row_sum(images[3] * start_turned)]
    late += [row_sum(images[i] * images[2]) for i in (0, 1)]
    late += [row_sum(images[i] * images[3]) for i in (0, 1, 2)]
    late += [row_sum(turned[i] * images[2]) for i in (0, 1)]
    late += [row_sum(turned[i] * images[3]) for i in (0, 1, 2)]
    dense = jnp.concatenate([early, row_of(late[:8], 0), row_of(late[8:], 0)], axis=0)

    wait_peers(t_in, nt - 1 - my_t)
    send_to_all(t, t_peers, dense, t_buf, sum_send.at[1], sum_recv.at[1])
    turned.append(times_i(images[3]))
    basis_turned = [times_i(field) for field in basis]
    sums_of(1, t_buf, nt, t_peers[0]).wait_recv()
    dense = jnp.sum(t_buf[...], axis=0)
    send_to_all(me_zx, zx_peers, dense, zx_buf, sum_send.at[2], sum_recv.at[2])
    sums_of(2, zx_buf, nz * nx, zx_peers[0]).wait_recv()
    dense = jnp.sum(zx_buf[...], axis=0)

    sums = []
    for g in range(3):
        spread = pltpu.roll(jnp.broadcast_to(dense[g : g + 1], (8, LANES)), 0, 1, stride=NRHS, stride_axis=0)
        sums += [spread[(8 - i) % 8 : (8 - i) % 8 + 1] for i in range(8)]
    diag = sums[0:2] + sums[8:10]
    right = [(sums[2], sums[4]), (sums[3], sums[5]), (sums[10], sums[12]), (sums[11], sums[13])]
    upper = {
        (0, 1): (sums[6], sums[7]),
        (0, 2): (sums[14], sums[19]),
        (1, 2): (sums[15], sums[20]),
        (0, 3): (sums[16], sums[21]),
        (1, 3): (sums[17], sums[22]),
        (2, 3): (sums[18], sums[23]),
    }
    coef = [(both_halves(c[0]), both_halves(c[1])) for c in solve(diag, upper, right)]

    field = None
    remain = start
    for k in range(4):
        cr, ci = coef[k]
        term = (cr * basis[k] + ci * basis_turned[k]) * inverse
        field = term if field is None else field + term
        remain = remain - cr * images[k] - ci * turned[k]
    x_ref[...] = field
    r_ref[...] = remain

    transfers(links_v.at[pl.ds(3, 4)], ball_peers[1], links_send, links_recv).wait_send()
    ball_transfers(0).wait_send()
    ball_transfers(1).wait_send()
    sums_of(0, theta_buf, nz * nx, zx_peers[0]).wait_send()
    sums_of(1, t_buf, nt, t_peers[0]).wait_send()
    sums_of(2, zx_buf, nz * nx, zx_peers[0]).wait_send()


def prolong_kernel(x_ref, r_ref, basis_ref, out_ref, remain_ref, rows_v):
    x = x_ref[...].astype(BF16).astype(F32)
    upper, lower = x[:NVEC], x[NVEC:]
    every = upper + pltpu.roll(upper, NRHS, 1) + pltpu.roll(lower, 2 * NRHS, 1) + pltpu.roll(lower, 3 * NRHS, 1)
    every = jnp.concatenate([every, times_i(every)], axis=0)
    group = group_of(every.shape)
    for s in range(4):
        rows_v[pl.ds(s, 2 * NVEC, stride=4), :] = jnp.where(group == s, every, 0.0)
    weights = rows_v[...].T.astype(BF16)
    for colour in range(3):
        value = jnp.dot(weights, basis_ref[colour], preferred_element_type=F32)
        out_ref[:, :, colour] = value.astype(BF16).reshape(2, 4, NRHS, 512)
    turned = r_ref[...].T
    remain_ref[0] = turned[0:NRHS]
    remain_ref[1] = turned[64 : 64 + NRHS]


def body(sizes, residual, null_vectors, coarse_op):
    sites = residual.shape[-1]
    res = residual.reshape(2, 4, 3, NRHS, sites)
    nv = null_vectors.transpose(0, 1, 3, 4, 5, 6, 2, 7).reshape(2, NVEC, 3, 4, sites)
    nt, nz, nx = sizes
    any_spec = pl.BlockSpec(memory_space=pltpu.HBM)
    vmem_spec = pl.BlockSpec(memory_space=pltpu.VMEM)
    field = jax.ShapeDtypeStruct((CDOF, LANES), F32)
    far = [pltpu.with_memory_space_constraint(a, pltpu.HBM) for a in (res, nv, coarse_op)]
    x, r, basis = pl.pallas_call(
        functools.partial(coarse_kernel, sizes),
        out_shape=(field, field, jax.ShapeDtypeStruct((3, 2 * NVEC * 4, sites), BF16)),
        in_specs=[any_spec] * 3,
        out_specs=(vmem_spec,) * 3,
        scratch_shapes=[
            pltpu.VMEM((3, 2, 4, NRHS, sites), BF16),
            pltpu.VMEM((3, 2, NVEC, 4, sites), BF16),
            pltpu.VMEM((3, LINKS, 2, CDOF, CDOF), BF16),
            pltpu.VMEM((nt, 2, CDOF, CDOF), BF16),
            pltpu.VMEM((2 * NVEC * 4, LANES), F32),
            pltpu.VMEM((7, 2 * CDOF, 8 * CDOF), BF16),
            pltpu.VMEM((2, len(ball(sizes)[1]), CDOF, LANES), BF16),
            pltpu.VMEM((nz * nx, 3, LANES), F32),
            pltpu.VMEM((nt, 3, LANES), F32),
            pltpu.VMEM((nz * nx, 3, LANES), F32),
            pltpu.SemaphoreType.DMA((10,)),
            pltpu.SemaphoreType.DMA((3,)),
            pltpu.SemaphoreType.DMA((3,)),
            pltpu.SemaphoreType.REGULAR,
            pltpu.SemaphoreType.REGULAR,
            pltpu.SemaphoreType.DMA,
            pltpu.SemaphoreType.DMA,
            pltpu.SemaphoreType.DMA((2,)),
            pltpu.SemaphoreType.DMA((2,)),
        ],
        compiler_params=pltpu.CompilerParams(
            collective_id=0, has_side_effects=True, vmem_limit_bytes=16 * 1024 * 1024
        ),
    )(*far)
    correction, remain = pl.pallas_call(
        prolong_kernel,
        out_shape=(
            jax.ShapeDtypeStruct((2, 4, 3, NRHS, sites), BF16),
            jax.ShapeDtypeStruct((2, NRHS, CDOF), F32),
        ),
        in_specs=[vmem_spec] * 3,
        out_specs=(vmem_spec, vmem_spec),
        scratch_shapes=[pltpu.VMEM((2 * NVEC * 4, LANES), F32)],
        compiler_params=pltpu.CompilerParams(vmem_limit_bytes=16 * 1024 * 1024),
    )(x, r, basis)
    correction = correction.reshape(2, 4, 3, NRHS, 1, 1, 1, sites)
    remain = remain.transpose(0, 2, 1).reshape(2, CDOF, 1, 1, 1, NRHS)
    return correction, remain


def solution(mesh):
    sizes = (mesh.shape["ta"], mesh.shape["gz"], mesh.shape["gy"])
    return jax.shard_map(
        functools.partial(body, sizes),
        mesh=mesh,
        in_specs=(
            P(None, None, None, None, "ta", "gz", "gy", None),
            P(None, None, None, None, "ta", "gz", "gy", None),
            P(None, "gz", "gy", None, None, None, None),
        ),
        out_specs=(
            P(None, None, None, None, "ta", "gz", "gy", None),
            P(None, None, "ta", "gz", "gy", None),
        ),
        check_vma=False,
    )
```

```python
import functools

import jax
import jax.numpy as jnp
from jax import lax
from jax.experimental import pallas as pl
from jax.experimental.pallas import tpu as pltpu
from jax.sharding import PartitionSpec as P

MESH = pl.DeviceIdType.MESH
F32 = jnp.float32
BF16 = jnp.bfloat16
CDOF = 48
NVEC = 24
NRHS = 16
LINKS = 9
LANES = 128


def lane_iota(shape):
    return lax.broadcasted_iota(jnp.int32, shape, len(shape) - 1)


def group_of(shape):
    return lax.rem(lax.div(lane_iota(shape), NRHS), 4)


def sign_of(shape):
    return jnp.where(lane_iota(shape) < 64, -1.0, 1.0).astype(F32)


def times_i(field):
    return sign_of(field.shape) * pltpu.roll(field, 64, 1)


def restrict(loads, nv_ref, res_ref, basis_ref, rows_ref):
    total = None
    for colour in range(3):
        for load in loads[colour]:
            load.wait()
        basis = nv_ref[colour].reshape(2 * NVEC * 4, 512)
        basis_ref[colour] = basis
        source = res_ref[colour].reshape(2 * 4 * NRHS, 512)
        part = lax.dot_general(basis, source, (((1,), (1,)), ((), ())), preferred_element_type=F32)
        total = part if total is None else total + part
    rows_ref[...] = total
    by_spin = [rows_ref[pl.ds(s, 2 * NVEC, stride=4), :] for s in range(4)]
    group = group_of((2 * NVEC, LANES))
    halves = []
    for chirality in range(2):
        a, b = 2 * chirality, 2 * chirality + 1
        picked = jnp.where(group == a, by_spin[a], jnp.where(group == b, by_spin[b], 0.0))
        picked = picked + pltpu.roll(picked, LANES - NRHS, 1)
        if chirality == 1:
            picked = pltpu.roll(picked, LANES - 2 * NRHS, 1)
        halves.append(picked[:NVEC] - times_i(picked[NVEC:]))
    field = jnp.concatenate(halves, axis=0)
    return jnp.where(group == 0, field, 0.0)


def split(wide):
    group = group_of(wide.shape)
    high = wide.astype(BF16).astype(F32)
    return jnp.where(group == 0, high, jnp.where(group == 2, wide - high, 0.0)).astype(BF16)


def both_groups(field):
    return field + pltpu.roll(field, 2 * NRHS, 1)


def combine(product):
    real, imag = product[:CDOF], product[CDOF:]
    first = group_of(real.shape) == 0
    back, forth = LANES - 2 * NRHS, 2 * NRHS
    total = real + jnp.where(first, pltpu.roll(real, back, 1), pltpu.roll(real, forth, 1))
    cross = pltpu.roll(imag, 64, 1) + jnp.where(first, pltpu.roll(imag, forth, 1), pltpu.roll(imag, back, 1))
    return total + sign_of(real.shape) * cross


def first_group(wide):
    return jnp.where(group_of(wide.shape) == 0, wide, 0.0)


def row_sum(product):
    return jnp.sum(product, axis=0, keepdims=True)


def cmul(a, b):
    return a[0] * b[0] - a[1] * b[1], a[0] * b[1] + a[1] * b[0]


def cmul_conj(a, b):
    return a[0] * b[0] + a[1] * b[1], a[0] * b[1] - a[1] * b[0]


def csub(a, b):
    return a[0] - b[0], a[1] - b[1]


def solve(diag, upper, right):
    n = len(diag)
    d, inv, low = [], [], {}
    for j in range(n):
        value = diag[j]
        for k in range(j):
            value = value - d[k] * (low[j, k][0] ** 2 + low[j, k][1] ** 2)
        d.append(value)
        inv.append(1.0 / value)
        for i in range(j + 1, n):
            entry = (upper[j, i][0], -upper[j, i][1])
            for k in range(j):
                term = cmul_conj(low[j, k], low[i, k])
                entry = csub(entry, (d[k] * term[0], d[k] * term[1]))
            low[i, j] = (entry[0] * inv[j], entry[1] * inv[j])
    y = []
    for i in range(n):
        value = right[i]
        for k in range(i):
            value = csub(value, cmul(low[i, k], y[k]))
        y.append(value)
    c = [None] * n
    for i in reversed(range(n)):
        value = (y[i][0] * inv[i], y[i][1] * inv[i])
        for k in range(i + 1, n):
            value = csub(value, cmul_conj(low[k, i], c[k]))
        c[i] = value
    return c


def both_halves(row):
    row = jnp.where(lane_iota(row.shape) < NRHS, row, 0.0)
    return row + pltpu.roll(row, 64, 1)


def others(count, me):
    return [k + jnp.where(k >= me, 1, 0) for k in range(count - 1)]


def rank_of(t, nt):
    half = nt // 2
    y = lax.div(t, 2)
    r = jnp.where(y == 0, 0, jnp.where(y <= half // 2, 2 * y - 1, 2 * (half - y)))
    return 2 * r + lax.rem(t, 2)


def slab_of(rank, nt):
    half = nt // 2
    r = lax.div(rank, 2)
    y = jnp.where(lax.rem(r, 2) == 1, lax.div(r + 1, 2), lax.rem(half - lax.div(r, 2), half))
    return 2 * y + lax.rem(rank, 2)


def ball(sizes):
    steps = [(1, 0, 0), (-1, 0, 0), (0, 1, 0), (0, -1, 0), (0, 0, 1), (0, 0, -1)]
    found = [(0, 0, 0)] + [shifted((0, 0, 0), step, sizes) for step in steps]
    for a in steps:
        for b in steps:
            site = shifted(shifted((0, 0, 0), a, sizes), b, sizes)
            if site not in found:
                found.append(site)
    return steps, found


def shifted(site, step, sizes):
    return tuple((a + b) % n for a, b, n in zip(site, step, sizes))


def pack_links(op_ref):
    def rows(part):
        blocks = [op_ref[m, part].astype(F32) for m in range(LINKS)]
        own = blocks[0] + (blocks[7] + blocks[8])
        high = own.astype(BF16).astype(F32)
        return jnp.concatenate([high, own - high] + blocks[1:7], axis=1)

    return jnp.concatenate([rows(0), rows(1)], axis=0).astype(BF16)


def times_links(links, blocks):
    field = jnp.concatenate([blocks[0]] + blocks, axis=0)
    return combine(jnp.dot(links[...], field, preferred_element_type=F32))


def send_to_all(me, peers, value, buf, send_sem, recv_sem):
    buf[me] = value
    for peer in peers:
        pltpu.make_async_remote_copy(
            src_ref=buf.at[me],
            dst_ref=buf.at[me],
            send_sem=send_sem,
            recv_sem=recv_sem,
            device_id=peer,
            device_id_type=MESH,
        ).start()


def transfers(block, peer, send_sem, recv_sem):
    return pltpu.make_async_remote_copy(
        src_ref=block, dst_ref=block, send_sem=send_sem, recv_sem=recv_sem, device_id=peer, device_id_type=MESH
    )


def coarse_kernel(
    sizes,
    res_hbm,
    nv_hbm,
    op_hbm,
    x_ref,
    r_ref,
    basis_ref,
    res_v,
    nv_v,
    op_v,
    col_v,
    rows_v,
    links_v,
    ball_v,
    theta_buf,
    t_buf,
    zx_buf,
    local_sem,
    sum_send,
    sum_recv,
    t_in,
    zx_in,
    links_send,
    links_recv,
    ball_send,
    ball_recv,
):
    nt, nz, nx = sizes
    t, z, x = lax.axis_index("ta"), lax.axis_index("gz"), lax.axis_index("gy")
    me_zx = z * nx + x
    loads = [
        (
            pltpu.make_async_copy(nv_hbm.at[:, :, colour], nv_v.at[colour], local_sem.at[2 * colour]),
            pltpu.make_async_copy(res_hbm.at[:, :, colour], res_v.at[colour], local_sem.at[2 * colour + 1]),
        )
        for colour in range(3)
    ]
    op_loads = [
        pltpu.make_async_copy(op_hbm.at[slab, 0, 0], op_v.at[i], local_sem.at[6 + i])
        for i, slab in enumerate((t, lax.rem(t + 1, nt), lax.rem(t + nt - 1, nt)))
    ]
    col_load = pltpu.make_async_copy(op_hbm.at[:, 0, 0, 0], col_v, local_sem.at[9])
    steps, sites = ball(sizes)
    ball_peers = [
        (lax.rem(t + nt - a, nt), lax.rem(z + nz - b, nz), lax.rem(x + nx - c, nx)) for a, b, c in sites
    ]
    my_t, my_zx = rank_of(t, nt), me_zx

    def t_peer(rank):
        return slab_of(rank, nt), z, x

    def zx_peer(rank):
        return t, lax.div(rank, nx), lax.rem(rank, nx)

    def signal_peers(semaphore, peer, first, count):
        def step(rank, carry):
            pl.semaphore_signal(semaphore, inc=1, device_id=peer(rank), device_id_type=MESH)
            return carry

        lax.fori_loop(first, count, step, 0)

    def wait_peers(semaphore, count):
        @pl.when(count > 0)
        def _():
            pl.semaphore_wait(semaphore, count)

    barrier = pltpu.get_barrier_semaphore()
    op_loads[0].start()
    for pair in loads:
        for load in pair:
            load.start()
    for peer in ball_peers[1:]:
        pl.semaphore_signal(barrier, inc=1, device_id=peer, device_id_type=MESH)
    signal_peers(barrier, zx_peer, my_zx + 1, nz * nx)
    signal_peers(barrier, t_peer, my_t + 1, nt)
    t_peers = [t_peer(k) for k in others(nt, my_t)]
    zx_peers = [zx_peer(k) for k in others(nz * nx, my_zx)]

    for load in op_loads[1:]:
        load.start()
    col_load.start()

    op_loads[0].wait()
    links_v[0] = pack_links(op_v.at[0])
    start = restrict(loads, nv_v, res_v, basis_ref, rows_v)

    def send_ball(k, wide):
        ball_v[k, 0] = split(wide)
        for i in reversed(range(1, len(sites))):
            pltpu.make_async_remote_copy(
                src_ref=ball_v.at[k, 0],
                dst_ref=ball_v.at[k, i],
                send_sem=ball_send.at[k],
                recv_sem=ball_recv.at[k],
                device_id=ball_peers[i],
                device_id_type=MESH,
            ).start()

    def ball_transfers(k):
        block = ball_v.at[k, pl.ds(1, len(sites) - 1)]
        return transfers(block, ball_peers[1], ball_send.at[k], ball_recv.at[k])

    def apply_twice(k):
        ball_transfers(k).wait_recv()

        def block(site, step=(0, 0, 0)):
            return ball_v[k, sites.index(shifted(site, step, sizes))]

        parts = []
        for i in range(7):
            wide = times_links(links_v.at[i], [block(sites[i], step) for step in [(0, 0, 0)] + steps])
            parts.append(split(wide))
            if i == 0:
                once = wide
        return once, times_links(links_v.at[0], parts)

    def sums_of(k, buf, count, peer):
        return transfers(buf.at[pl.ds(0, count - 1)], peer, sum_send.at[k], sum_recv.at[k])

    pl.semaphore_wait(barrier, len(sites) - 1 + my_t + my_zx)
    send_ball(0, both_groups(start))
    for i in range(3, 7):
        pltpu.make_async_remote_copy(
            src_ref=links_v.at[0],
            dst_ref=links_v.at[i],
            send_sem=links_send,
            recv_sem=links_recv,
            device_id=ball_peers[i],
            device_id_type=MESH,
        ).start()
    signal_peers(zx_in, zx_peer, 0, my_zx)

    col_load.wait()
    eye = lax.broadcasted_iota(jnp.int32, (CDOF, CDOF), 0) == lax.broadcasted_iota(jnp.int32, (CDOF, CDOF), 1)
    trace = [jnp.zeros((CDOF, CDOF), F32), jnp.zeros((CDOF, CDOF), F32)]
    square = jnp.zeros((CDOF, CDOF), F32)
    for slab in range(nt):
        for part in range(2):
            block = col_v[slab, part].astype(F32)
            trace[part] = trace[part] + block
            square = square + block * block
    scale = 1.0 / (nt * nz * nx * CDOF)
    stats = [jnp.where(eye, trace[0], 0.0), jnp.where(eye, trace[1], 0.0), square]
    stats = [jnp.sum(row_sum(value), axis=1, keepdims=True) * scale for value in stats]
    place = lane_iota((1, LANES))
    stats = sum(jnp.where(place == i, value, 0.0) for i, value in enumerate(stats))

    for i in (1, 2):
        op_loads[i].wait()
        links_v[i] = pack_links(op_v.at[i])

    wait_peers(zx_in, nz * nx - 1 - my_zx)
    send_to_all(me_zx, zx_peers, stats, theta_buf, sum_send.at[0], sum_recv.at[0])
    transfers(links_v.at[pl.ds(3, 4)], ball_peers[1], links_send, links_recv).wait_recv()
    once, twice = apply_twice(0)
    send_ball(1, twice)
    signal_peers(t_in, t_peer, 0, my_t)
    powers = [start, first_group(once), first_group(twice)]

    sums_of(0, theta_buf, nz * nx, zx_peers[0]).wait_recv()
    stats = jnp.sum(theta_buf[...], axis=0)
    stats = [
        jnp.broadcast_to(jnp.sum(jnp.where(place == i, stats, 0.0), axis=1, keepdims=True), (1, LANES))
        for i in range(3)
    ]
    square = stats[2]
    inverse = jnp.where(square > 0.0, lax.rsqrt(jnp.where(square > 0.0, square, 1.0)), 1.0)
    theta = (stats[0] * inverse, stats[1] * inverse)
    weights = [inverse]
    for _ in range(3):
        weights.append(weights[-1] * inverse)

    def times_theta(field):
        return theta[0] * field + theta[1] * times_i(field)

    v1, v2 = powers[1] * weights[0], powers[2] * weights[1]
    one = [v1 - times_theta(start), v2 - times_theta(v1)]
    two = one[1] - times_theta(one[0])
    basis = [start, one[0], two]
    images = [v1, two + times_theta(one[0])]
    turned = [times_i(image) for image in images]
    start_turned = times_i(start)
    last_one, last_two, last_three = times_theta(v2), times_theta(one[1]), times_theta(two)

    def row_of(rows, first):
        table = jnp.concatenate(rows, axis=0)
        table = table + pltpu.roll(table, 64, 1)
        table = jnp.where(lane_iota(table.shape) < NRHS, table, 0.0)
        return row_sum(pltpu.roll(table, first * NRHS, 1, stride=NRHS, stride_axis=0))

    early = [row_sum(images[k] * images[k]) for k in range(2)]
    early += [row_sum(images[k] * start) for k in range(2)]
    early += [row_sum(turned[k] * start) for k in range(2)]
    early += [row_sum(images[0] * images[1]), row_sum(turned[0] * images[1])]
    early = row_of(early, 0)

    once, twice = apply_twice(1)
    v3, v4 = first_group(once) * weights[2], first_group(twice) * weights[3]

    one.append(v3 - last_one)
    two_next = one[2] - last_two
    basis.append(two_next - last_three)
    images.append(basis[3] + last_three)
    turned.append(times_i(images[2]))
    images.append(v4 - times_theta(v3) - times_theta(one[2]) - times_theta(two_next))
    late = [row_sum(images[k] * images[k]) for k in (2, 3)]
    late += [row_sum(images[k] * start) for k in (2, 3)]
    late += [row_sum(turned[2] * start), -row_sum(images[3] * start_turned)]
    late += [row_sum(images[i] * images[2]) for i in (0, 1)]
    late += [row_sum(images[i] * images[3]) for i in (0, 1, 2)]
    late += [row_sum(turned[i] * images[2]) for i in (0, 1)]
    late += [row_sum(turned[i] * images[3]) for i in (0, 1, 2)]
    dense = jnp.concatenate([early, row_of(late[:8], 0), row_of(late[8:], 0)], axis=0)

    wait_peers(t_in, nt - 1 - my_t)
    send_to_all(t, t_peers, dense, t_buf, sum_send.at[1], sum_recv.at[1])
    turned.append(times_i(images[3]))
    basis_turned = [times_i(field) for field in basis]
    sums_of(1, t_buf, nt, t_peers[0]).wait_recv()
    dense = jnp.sum(t_buf[...], axis=0)
    send_to_all(me_zx, zx_peers, dense, zx_buf, sum_send.at[2], sum_recv.at[2])
    sums_of(2, zx_buf, nz * nx, zx_peers[0]).wait_recv()
    dense = jnp.sum(zx_buf[...], axis=0)

    sums = []
    for g in range(3):
        spread = pltpu.roll(jnp.broadcast_to(dense[g : g + 1], (8, LANES)), 0, 1, stride=NRHS, stride_axis=0)
        sums += [spread[(8 - i) % 8 : (8 - i) % 8 + 1] for i in range(8)]
    diag = sums[0:2] + sums[8:10]
    right = [(sums[2], sums[4]), (sums[3], sums[5]), (sums[10], sums[12]), (sums[11], sums[13])]
    upper = {
        (0, 1): (sums[6], sums[7]),
        (0, 2): (sums[14], sums[19]),
        (1, 2): (sums[15], sums[20]),
        (0, 3): (sums[16], sums[21]),
        (1, 3): (sums[17], sums[22]),
        (2, 3): (sums[18], sums[23]),
    }
    coef = [(both_halves(c[0]), both_halves(c[1])) for c in solve(diag, upper, right)]

    field = None
    remain = start
    for k in range(4):
        cr, ci = coef[k]
        term = (cr * basis[k] + ci * basis_turned[k]) * inverse
        field = term if field is None else field + term
        remain = remain - cr * images[k] - ci * turned[k]
    x_ref[...] = field
    r_ref[...] = remain

    transfers(links_v.at[pl.ds(3, 4)], ball_peers[1], links_send, links_recv).wait_send()
    ball_transfers(0).wait_send()
    ball_transfers(1).wait_send()
    sums_of(0, theta_buf, nz * nx, zx_peers[0]).wait_send()
    sums_of(1, t_buf, nt, t_peers[0]).wait_send()
    sums_of(2, zx_buf, nz * nx, zx_peers[0]).wait_send()


def prolong_kernel(x_ref, r_ref, basis_ref, out_ref, remain_ref, rows_v):
    x = x_ref[...].astype(BF16).astype(F32)
    upper, lower = x[:NVEC], x[NVEC:]
    every = upper + pltpu.roll(upper, NRHS, 1) + pltpu.roll(lower, 2 * NRHS, 1) + pltpu.roll(lower, 3 * NRHS, 1)
    every = jnp.concatenate([every, times_i(every)], axis=0)
    group = group_of(every.shape)
    for s in range(4):
        rows_v[pl.ds(s, 2 * NVEC, stride=4), :] = jnp.where(group == s, every, 0.0)
    weights = rows_v[...].T.astype(BF16)
    for colour in range(3):
        value = jnp.dot(weights, basis_ref[colour], preferred_element_type=F32)
        out_ref[:, :, colour] = value.astype(BF16).reshape(2, 4, NRHS, 512)
    turned = r_ref[...].T
    remain_ref[0] = turned[0:NRHS]
    remain_ref[1] = turned[64 : 64 + NRHS]


def body(sizes, residual, null_vectors, coarse_op):
    sites = residual.shape[-1]
    res = residual.reshape(2, 4, 3, NRHS, sites)
    nv = null_vectors.transpose(0, 1, 3, 4, 5, 6, 2, 7).reshape(2, NVEC, 3, 4, sites)
    nt, nz, nx = sizes
    any_spec = pl.BlockSpec(memory_space=pltpu.HBM)
    vmem_spec = pl.BlockSpec(memory_space=pltpu.VMEM)
    field = jax.ShapeDtypeStruct((CDOF, LANES), F32)
    far = [pltpu.with_memory_space_constraint(a, pltpu.HBM) for a in (res, nv, coarse_op)]
    x, r, basis = pl.pallas_call(
        functools.partial(coarse_kernel, sizes),
        out_shape=(field, field, jax.ShapeDtypeStruct((3, 2 * NVEC * 4, sites), BF16)),
        in_specs=[any_spec] * 3,
        out_specs=(vmem_spec,) * 3,
        scratch_shapes=[
            pltpu.VMEM((3, 2, 4, NRHS, sites), BF16),
            pltpu.VMEM((3, 2, NVEC, 4, sites), BF16),
            pltpu.VMEM((3, LINKS, 2, CDOF, CDOF), BF16),
            pltpu.VMEM((nt, 2, CDOF, CDOF), BF16),
            pltpu.VMEM((2 * NVEC * 4, LANES), F32),
            pltpu.VMEM((7, 2 * CDOF, 8 * CDOF), BF16),
            pltpu.VMEM((2, len(ball(sizes)[1]), CDOF, LANES), BF16),
            pltpu.VMEM((nz * nx, 1, LANES), F32),
            pltpu.VMEM((nt, 3, LANES), F32),
            pltpu.VMEM((nz * nx, 3, LANES), F32),
            pltpu.SemaphoreType.DMA((10,)),
            pltpu.SemaphoreType.DMA((3,)),
            pltpu.SemaphoreType.DMA((3,)),
            pltpu.SemaphoreType.REGULAR,
            pltpu.SemaphoreType.REGULAR,
            pltpu.SemaphoreType.DMA,
            pltpu.SemaphoreType.DMA,
            pltpu.SemaphoreType.DMA((2,)),
            pltpu.SemaphoreType.DMA((2,)),
        ],
        compiler_params=pltpu.CompilerParams(
            collective_id=0, has_side_effects=True, vmem_limit_bytes=16 * 1024 * 1024
        ),
    )(*far)
    correction, remain = pl.pallas_call(
        prolong_kernel,
        out_shape=(
            jax.ShapeDtypeStruct((2, 4, 3, NRHS, sites), BF16),
            jax.ShapeDtypeStruct((2, NRHS, CDOF), F32),
        ),
        in_specs=[vmem_spec] * 3,
        out_specs=(vmem_spec, vmem_spec),
        scratch_shapes=[pltpu.VMEM((2 * NVEC * 4, LANES), F32)],
        compiler_params=pltpu.CompilerParams(vmem_limit_bytes=16 * 1024 * 1024),
    )(x, r, basis)
    correction = correction.reshape(2, 4, 3, NRHS, 1, 1, 1, sites)
    remain = remain.transpose(0, 2, 1).reshape(2, CDOF, 1, 1, 1, NRHS)
    return correction, remain


def solution(mesh):
    sizes = (mesh.shape["ta"], mesh.shape["gz"], mesh.shape["gy"])
    return jax.shard_map(
        functools.partial(body, sizes),
        mesh=mesh,
        in_specs=(
            P(None, None, None, None, "ta", "gz", "gy", None),
            P(None, None, None, None, "ta", "gz", "gy", None),
            P(None, "gz", "gy", None, None, None, None),
        ),
        out_specs=(
            P(None, None, None, None, "ta", "gz", "gy", None),
            P(None, None, "ta", "gz", "gy", None),
        ),
        check_vma=False,
    )
```

```python
import functools

import jax
import jax.numpy as jnp
from jax import lax
from jax.experimental import pallas as pl
from jax.experimental.pallas import tpu as pltpu
from jax.sharding import PartitionSpec as P

MESH = pl.DeviceIdType.MESH
F32 = jnp.float32
BF16 = jnp.bfloat16
CDOF = 48
NVEC = 24
NRHS = 16
LINKS = 9
LANES = 128


def lane_iota(shape):
    return lax.broadcasted_iota(jnp.int32, shape, len(shape) - 1)


def group_of(shape):
    return lax.rem(lax.div(lane_iota(shape), NRHS), 4)


def sign_of(shape):
    return jnp.where(lane_iota(shape) < 64, -1.0, 1.0).astype(F32)


def times_i(field):
    return sign_of(field.shape) * pltpu.roll(field, 64, 1)


def restrict(loads, nv_ref, res_ref, basis_ref, rows_ref):
    total = None
    for colour in range(3):
        for load in loads[colour]:
            load.wait()
        basis = nv_ref[colour].reshape(2 * NVEC * 4, 512)
        basis_ref[colour] = basis
        source = res_ref[colour].reshape(2 * 4 * NRHS, 512)
        part = lax.dot_general(basis, source, (((1,), (1,)), ((), ())), preferred_element_type=F32)
        total = part if total is None else total + part
    rows_ref[...] = total
    by_spin = [rows_ref[pl.ds(s, 2 * NVEC, stride=4), :] for s in range(4)]
    group = group_of((2 * NVEC, LANES))
    halves = []
    for chirality in range(2):
        a, b = 2 * chirality, 2 * chirality + 1
        picked = jnp.where(group == a, by_spin[a], jnp.where(group == b, by_spin[b], 0.0))
        picked = picked + pltpu.roll(picked, LANES - NRHS, 1)
        if chirality == 1:
            picked = pltpu.roll(picked, LANES - 2 * NRHS, 1)
        halves.append(picked[:NVEC] - times_i(picked[NVEC:]))
    field = jnp.concatenate(halves, axis=0)
    return jnp.where(group == 0, field, 0.0)


def split(wide):
    group = group_of(wide.shape)
    high = wide.astype(BF16).astype(F32)
    return jnp.where(group == 0, high, jnp.where(group == 2, wide - high, 0.0)).astype(BF16)


def both_groups(field):
    return field + pltpu.roll(field, 2 * NRHS, 1)


def combine(product):
    real, imag = product[:CDOF], product[CDOF:]
    first = group_of(real.shape) == 0
    back, forth = LANES - 2 * NRHS, 2 * NRHS
    total = real + jnp.where(first, pltpu.roll(real, back, 1), pltpu.roll(real, forth, 1))
    cross = pltpu.roll(imag, 64, 1) + jnp.where(first, pltpu.roll(imag, forth, 1), pltpu.roll(imag, back, 1))
    return total + sign_of(real.shape) * cross


def first_group(wide):
    return jnp.where(group_of(wide.shape) == 0, wide, 0.0)


def row_sum(product):
    return jnp.sum(product, axis=0, keepdims=True)


def cmul(a, b):
    return a[0] * b[0] - a[1] * b[1], a[0] * b[1] + a[1] * b[0]


def cmul_conj(a, b):
    return a[0] * b[0] + a[1] * b[1], a[0] * b[1] - a[1] * b[0]


def csub(a, b):
    return a[0] - b[0], a[1] - b[1]


def solve(diag, upper, right):
    n = len(diag)
    d, inv, low = [], [], {}
    for j in range(n):
        value = diag[j]
        for k in range(j):
            value = value - d[k] * (low[j, k][0] ** 2 + low[j, k][1] ** 2)
        d.append(value)
        inv.append(1.0 / value)
        for i in range(j + 1, n):
            entry = (upper[j, i][0], -upper[j, i][1])
            for k in range(j):
                term = cmul_conj(low[j, k], low[i, k])
                entry = csub(entry, (d[k] * term[0], d[k] * term[1]))
            low[i, j] = (entry[0] * inv[j], entry[1] * inv[j])
    y = []
    for i in range(n):
        value = right[i]
        for k in range(i):
            value = csub(value, cmul(low[i, k], y[k]))
        y.append(value)
    c = [None] * n
    for i in reversed(range(n)):
        value = (y[i][0] * inv[i], y[i][1] * inv[i])
        for k in range(i + 1, n):
            value = csub(value, cmul_conj(low[k, i], c[k]))
        c[i] = value
    return c


def both_halves(row):
    row = jnp.where(lane_iota(row.shape) < NRHS, row, 0.0)
    return row + pltpu.roll(row, 64, 1)


def others(count, me):
    return [k + jnp.where(k >= me, 1, 0) for k in range(count - 1)]


def rank_of(t, nt):
    half = nt // 2
    y = lax.div(t, 2)
    r = jnp.where(y == 0, 0, jnp.where(y <= half // 2, 2 * y - 1, 2 * (half - y)))
    return 2 * r + lax.rem(t, 2)


def slab_of(rank, nt):
    half = nt // 2
    r = lax.div(rank, 2)
    y = jnp.where(lax.rem(r, 2) == 1, lax.div(r + 1, 2), lax.rem(half - lax.div(r, 2), half))
    return 2 * y + lax.rem(rank, 2)


def ball(sizes):
    steps = [(1, 0, 0), (-1, 0, 0), (0, 1, 0), (0, -1, 0), (0, 0, 1), (0, 0, -1)]
    found = [(0, 0, 0)] + [shifted((0, 0, 0), step, sizes) for step in steps]
    for a in steps:
        for b in steps:
            site = shifted(shifted((0, 0, 0), a, sizes), b, sizes)
            if site not in found:
                found.append(site)
    return steps, found


def shifted(site, step, sizes):
    return tuple((a + b) % n for a, b, n in zip(site, step, sizes))


def pack_links(op_ref):
    def rows(part):
        blocks = [op_ref[m, part].astype(F32) for m in range(LINKS)]
        own = blocks[0] + (blocks[7] + blocks[8])
        high = own.astype(BF16).astype(F32)
        return jnp.concatenate([high, own - high] + blocks[1:7], axis=1)

    return jnp.concatenate([rows(0), rows(1)], axis=0).astype(BF16)


def times_links(links, blocks):
    field = jnp.concatenate([blocks[0]] + blocks, axis=0)
    return combine(jnp.dot(links[...], field, preferred_element_type=F32))


def send_to_all(me, peers, value, buf, send_sem, recv_sem):
    buf[me] = value
    for peer in peers:
        pltpu.make_async_remote_copy(
            src_ref=buf.at[me],
            dst_ref=buf.at[me],
            send_sem=send_sem,
            recv_sem=recv_sem,
            device_id=peer,
            device_id_type=MESH,
        ).start()


def transfers(block, peer, send_sem, recv_sem):
    return pltpu.make_async_remote_copy(
        src_ref=block, dst_ref=block, send_sem=send_sem, recv_sem=recv_sem, device_id=peer, device_id_type=MESH
    )


def coarse_kernel(
    sizes,
    res_hbm,
    nv_hbm,
    op_hbm,
    x_ref,
    r_ref,
    basis_ref,
    res_v,
    nv_v,
    op_v,
    col_v,
    rows_v,
    links_v,
    ball_v,
    theta_buf,
    t_buf,
    zx_buf,
    local_sem,
    sum_send,
    sum_recv,
    t_in,
    zx_in,
    links_send,
    links_recv,
    ball_send,
    ball_recv,
):
    nt, nz, nx = sizes
    t, z, x = lax.axis_index("ta"), lax.axis_index("gz"), lax.axis_index("gy")
    me_zx = z * nx + x
    loads = [
        (
            pltpu.make_async_copy(nv_hbm.at[:, :, colour], nv_v.at[colour], local_sem.at[2 * colour]),
            pltpu.make_async_copy(res_hbm.at[:, :, colour], res_v.at[colour], local_sem.at[2 * colour + 1]),
        )
        for colour in range(3)
    ]
    op_loads = [
        pltpu.make_async_copy(op_hbm.at[slab, 0, 0], op_v.at[i], local_sem.at[6 + i])
        for i, slab in enumerate((t, lax.rem(t + 1, nt), lax.rem(t + nt - 1, nt)))
    ]
    col_load = pltpu.make_async_copy(op_hbm.at[:, 0, 0, 0], col_v, local_sem.at[9])
    steps, sites = ball(sizes)
    ball_peers = [
        (lax.rem(t + nt - a, nt), lax.rem(z + nz - b, nz), lax.rem(x + nx - c, nx)) for a, b, c in sites
    ]
    my_t, my_zx = rank_of(t, nt), me_zx

    def t_peer(rank):
        return slab_of(rank, nt), z, x

    def zx_peer(rank):
        return t, lax.div(rank, nx), lax.rem(rank, nx)

    def signal_peers(semaphore, peer, first, count):
        def step(rank, carry):
            pl.semaphore_signal(semaphore, inc=1, device_id=peer(rank), device_id_type=MESH)
            return carry

        lax.fori_loop(first, count, step, 0)

    def wait_peers(semaphore, count):
        @pl.when(count > 0)
        def _():
            pl.semaphore_wait(semaphore, count)

    barrier = pltpu.get_barrier_semaphore()
    op_loads[0].start()
    for pair in loads:
        for load in pair:
            load.start()
    for peer in ball_peers[1:]:
        pl.semaphore_signal(barrier, inc=1, device_id=peer, device_id_type=MESH)
    signal_peers(barrier, zx_peer, my_zx + 1, nz * nx)
    signal_peers(barrier, t_peer, my_t + 1, nt)
    t_peers = [t_peer(k) for k in others(nt, my_t)]
    zx_peers = [zx_peer(k) for k in others(nz * nx, my_zx)]


    op_loads[0].wait()
    links_v[0] = pack_links(op_v.at[0])
    start = restrict(loads, nv_v, res_v, basis_ref, rows_v)

    def send_ball(k, wide):
        ball_v[k, 0] = split(wide)
        for i in reversed(range(1, len(sites))):
            pltpu.make_async_remote_copy(
                src_ref=ball_v.at[k, 0],
                dst_ref=ball_v.at[k, i],
                send_sem=ball_send.at[k],
                recv_sem=ball_recv.at[k],
                device_id=ball_peers[i],
                device_id_type=MESH,
            ).start()

    def ball_transfers(k):
        block = ball_v.at[k, pl.ds(1, len(sites) - 1)]
        return transfers(block, ball_peers[1], ball_send.at[k], ball_recv.at[k])

    def apply_twice(k):
        ball_transfers(k).wait_recv()

        def block(site, step=(0, 0, 0)):
            return ball_v[k, sites.index(shifted(site, step, sizes))]

        parts = []
        for i in range(7):
            wide = times_links(links_v.at[i], [block(sites[i], step) for step in [(0, 0, 0)] + steps])
            parts.append(split(wide))
            if i == 0:
                once = wide
        return once, times_links(links_v.at[0], parts)

    def sums_of(k, buf, count, peer):
        return transfers(buf.at[pl.ds(0, count - 1)], peer, sum_send.at[k], sum_recv.at[k])

    pl.semaphore_wait(barrier, len(sites) - 1 + my_t + my_zx)
    col_load.start()
    for load in op_loads[1:]:
        load.start()
    send_ball(0, both_groups(start))
    for i in range(3, 7):
        pltpu.make_async_remote_copy(
            src_ref=links_v.at[0],
            dst_ref=links_v.at[i],
            send_sem=links_send,
            recv_sem=links_recv,
            device_id=ball_peers[i],
            device_id_type=MESH,
        ).start()
    signal_peers(zx_in, zx_peer, 0, my_zx)

    col_load.wait()
    eye = lax.broadcasted_iota(jnp.int32, (CDOF, CDOF), 0) == lax.broadcasted_iota(jnp.int32, (CDOF, CDOF), 1)
    trace = [jnp.zeros((CDOF, CDOF), F32), jnp.zeros((CDOF, CDOF), F32)]
    square = jnp.zeros((CDOF, CDOF), F32)
    for slab in range(nt):
        for part in range(2):
            block = col_v[slab, part].astype(F32)
            trace[part] = trace[part] + block
            square = square + block * block
    scale = 1.0 / (nt * nz * nx * CDOF)
    stats = [jnp.where(eye, trace[0], 0.0), jnp.where(eye, trace[1], 0.0), square]
    stats = [jnp.sum(row_sum(value), axis=1, keepdims=True) * scale for value in stats]
    place = lane_iota((1, LANES))
    stats = sum(jnp.where(place == i, value, 0.0) for i, value in enumerate(stats))

    for i in (1, 2):
        op_loads[i].wait()
        links_v[i] = pack_links(op_v.at[i])

    wait_peers(zx_in, nz * nx - 1 - my_zx)
    send_to_all(me_zx, zx_peers, stats, theta_buf, sum_send.at[0], sum_recv.at[0])
    transfers(links_v.at[pl.ds(3, 4)], ball_peers[1], links_send, links_recv).wait_recv()
    once, twice = apply_twice(0)
    send_ball(1, twice)
    signal_peers(t_in, t_peer, 0, my_t)
    powers = [start, first_group(once), first_group(twice)]

    sums_of(0, theta_buf, nz * nx, zx_peers[0]).wait_recv()
    stats = jnp.sum(theta_buf[...], axis=0)
    stats = [
        jnp.broadcast_to(jnp.sum(jnp.where(place == i, stats, 0.0), axis=1, keepdims=True), (1, LANES))
        for i in range(3)
    ]
    square = stats[2]
    inverse = jnp.where(square > 0.0, lax.rsqrt(jnp.where(square > 0.0, square, 1.0)), 1.0)
    theta = (stats[0] * inverse, stats[1] * inverse)
    weights = [inverse]
    for _ in range(3):
        weights.append(weights[-1] * inverse)

    def times_theta(field):
        return theta[0] * field + theta[1] * times_i(field)

    v1, v2 = powers[1] * weights[0], powers[2] * weights[1]
    one = [v1 - times_theta(start), v2 - times_theta(v1)]
    two = one[1] - times_theta(one[0])
    basis = [start, one[0], two]
    images = [v1, two + times_theta(one[0])]
    turned = [times_i(image) for image in images]
    start_turned = times_i(start)
    last_one, last_two, last_three = times_theta(v2), times_theta(one[1]), times_theta(two)

    def row_of(rows, first):
        table = jnp.concatenate(rows, axis=0)
        table = table + pltpu.roll(table, 64, 1)
        table = jnp.where(lane_iota(table.shape) < NRHS, table, 0.0)
        return row_sum(pltpu.roll(table, first * NRHS, 1, stride=NRHS, stride_axis=0))

    early = [row_sum(images[k] * images[k]) for k in range(2)]
    early += [row_sum(images[k] * start) for k in range(2)]
    early += [row_sum(turned[k] * start) for k in range(2)]
    early += [row_sum(images[0] * images[1]), row_sum(turned[0] * images[1])]
    early = row_of(early, 0)

    once, twice = apply_twice(1)
    v3, v4 = first_group(once) * weights[2], first_group(twice) * weights[3]

    one.append(v3 - last_one)
    two_next = one[2] - last_two
    basis.append(two_next - last_three)
    images.append(basis[3] + last_three)
    turned.append(times_i(images[2]))
    images.append(v4 - times_theta(v3) - times_theta(one[2]) - times_theta(two_next))
    late = [row_sum(images[k] * images[k]) for k in (2, 3)]
    late += [row_sum(images[k] * start) for k in (2, 3)]
    late += [row_sum(turned[2] * start), -row_sum(images[3] * start_turned)]
    late += [row_sum(images[i] * images[2]) for i in (0, 1)]
    late += [row_sum(images[i] * images[3]) for i in (0, 1, 2)]
    late += [row_sum(turned[i] * images[2]) for i in (0, 1)]
    late += [row_sum(turned[i] * images[3]) for i in (0, 1, 2)]
    dense = jnp.concatenate([early, row_of(late[:8], 0), row_of(late[8:], 0)], axis=0)

    wait_peers(t_in, nt - 1 - my_t)
    send_to_all(t, t_peers, dense, t_buf, sum_send.at[1], sum_recv.at[1])
    turned.append(times_i(images[3]))
    basis_turned = [times_i(field) for field in basis]
    sums_of(1, t_buf, nt, t_peers[0]).wait_recv()
    dense = jnp.sum(t_buf[...], axis=0)
    send_to_all(me_zx, zx_peers, dense, zx_buf, sum_send.at[2], sum_recv.at[2])
    sums_of(2, zx_buf, nz * nx, zx_peers[0]).wait_recv()
    dense = jnp.sum(zx_buf[...], axis=0)

    sums = []
    for g in range(3):
        spread = pltpu.roll(jnp.broadcast_to(dense[g : g + 1], (8, LANES)), 0, 1, stride=NRHS, stride_axis=0)
        sums += [spread[(8 - i) % 8 : (8 - i) % 8 + 1] for i in range(8)]
    diag = sums[0:2] + sums[8:10]
    right = [(sums[2], sums[4]), (sums[3], sums[5]), (sums[10], sums[12]), (sums[11], sums[13])]
    upper = {
        (0, 1): (sums[6], sums[7]),
        (0, 2): (sums[14], sums[19]),
        (1, 2): (sums[15], sums[20]),
        (0, 3): (sums[16], sums[21]),
        (1, 3): (sums[17], sums[22]),
        (2, 3): (sums[18], sums[23]),
    }
    coef = [(both_halves(c[0]), both_halves(c[1])) for c in solve(diag, upper, right)]

    field = None
    remain = start
    for k in range(4):
        cr, ci = coef[k]
        term = (cr * basis[k] + ci * basis_turned[k]) * inverse
        field = term if field is None else field + term
        remain = remain - cr * images[k] - ci * turned[k]
    x_ref[...] = field
    r_ref[...] = remain

    transfers(links_v.at[pl.ds(3, 4)], ball_peers[1], links_send, links_recv).wait_send()
    ball_transfers(0).wait_send()
    ball_transfers(1).wait_send()
    sums_of(0, theta_buf, nz * nx, zx_peers[0]).wait_send()
    sums_of(1, t_buf, nt, t_peers[0]).wait_send()
    sums_of(2, zx_buf, nz * nx, zx_peers[0]).wait_send()


def prolong_kernel(x_ref, r_ref, basis_ref, out_ref, remain_ref, rows_v):
    x = x_ref[...].astype(BF16).astype(F32)
    upper, lower = x[:NVEC], x[NVEC:]
    every = upper + pltpu.roll(upper, NRHS, 1) + pltpu.roll(lower, 2 * NRHS, 1) + pltpu.roll(lower, 3 * NRHS, 1)
    every = jnp.concatenate([every, times_i(every)], axis=0)
    group = group_of(every.shape)
    for s in range(4):
        rows_v[pl.ds(s, 2 * NVEC, stride=4), :] = jnp.where(group == s, every, 0.0)
    weights = rows_v[...].T.astype(BF16)
    for colour in range(3):
        value = jnp.dot(weights, basis_ref[colour], preferred_element_type=F32)
        out_ref[:, :, colour] = value.astype(BF16).reshape(2, 4, NRHS, 512)
    turned = r_ref[...].T
    remain_ref[0] = turned[0:NRHS]
    remain_ref[1] = turned[64 : 64 + NRHS]


def body(sizes, residual, null_vectors, coarse_op):
    sites = residual.shape[-1]
    res = residual.reshape(2, 4, 3, NRHS, sites)
    nv = null_vectors.transpose(0, 1, 3, 4, 5, 6, 2, 7).reshape(2, NVEC, 3, 4, sites)
    nt, nz, nx = sizes
    any_spec = pl.BlockSpec(memory_space=pltpu.HBM)
    vmem_spec = pl.BlockSpec(memory_space=pltpu.VMEM)
    field = jax.ShapeDtypeStruct((CDOF, LANES), F32)
    far = [pltpu.with_memory_space_constraint(a, pltpu.HBM) for a in (res, nv, coarse_op)]
    x, r, basis = pl.pallas_call(
        functools.partial(coarse_kernel, sizes),
        out_shape=(field, field, jax.ShapeDtypeStruct((3, 2 * NVEC * 4, sites), BF16)),
        in_specs=[any_spec] * 3,
        out_specs=(vmem_spec,) * 3,
        scratch_shapes=[
            pltpu.VMEM((3, 2, 4, NRHS, sites), BF16),
            pltpu.VMEM((3, 2, NVEC, 4, sites), BF16),
            pltpu.VMEM((3, LINKS, 2, CDOF, CDOF), BF16),
            pltpu.VMEM((nt, 2, CDOF, CDOF), BF16),
            pltpu.VMEM((2 * NVEC * 4, LANES), F32),
            pltpu.VMEM((7, 2 * CDOF, 8 * CDOF), BF16),
            pltpu.VMEM((2, len(ball(sizes)[1]), CDOF, LANES), BF16),
            pltpu.VMEM((nz * nx, 1, LANES), F32),
            pltpu.VMEM((nt, 3, LANES), F32),
            pltpu.VMEM((nz * nx, 3, LANES), F32),
            pltpu.SemaphoreType.DMA((10,)),
            pltpu.SemaphoreType.DMA((3,)),
            pltpu.SemaphoreType.DMA((3,)),
            pltpu.SemaphoreType.REGULAR,
            pltpu.SemaphoreType.REGULAR,
            pltpu.SemaphoreType.DMA,
            pltpu.SemaphoreType.DMA,
            pltpu.SemaphoreType.DMA((2,)),
            pltpu.SemaphoreType.DMA((2,)),
        ],
        compiler_params=pltpu.CompilerParams(
            collective_id=0, has_side_effects=True, vmem_limit_bytes=16 * 1024 * 1024
        ),
    )(*far)
    correction, remain = pl.pallas_call(
        prolong_kernel,
        out_shape=(
            jax.ShapeDtypeStruct((2, 4, 3, NRHS, sites), BF16),
            jax.ShapeDtypeStruct((2, NRHS, CDOF), F32),
        ),
        in_specs=[vmem_spec] * 3,
        out_specs=(vmem_spec, vmem_spec),
        scratch_shapes=[pltpu.VMEM((2 * NVEC * 4, LANES), F32)],
        compiler_params=pltpu.CompilerParams(vmem_limit_bytes=16 * 1024 * 1024),
    )(x, r, basis)
    correction = correction.reshape(2, 4, 3, NRHS, 1, 1, 1, sites)
    remain = remain.transpose(0, 2, 1).reshape(2, CDOF, 1, 1, 1, NRHS)
    return correction, remain


def solution(mesh):
    sizes = (mesh.shape["ta"], mesh.shape["gz"], mesh.shape["gy"])
    return jax.shard_map(
        functools.partial(body, sizes),
        mesh=mesh,
        in_specs=(
            P(None, None, None, None, "ta", "gz", "gy", None),
            P(None, None, None, None, "ta", "gz", "gy", None),
            P(None, "gz", "gy", None, None, None, None),
        ),
        out_specs=(
            P(None, None, None, None, "ta", "gz", "gy", None),
            P(None, None, "ta", "gz", "gy", None),
        ),
        check_vma=False,
    )
```
